32 devices in a mesh: group: 4 (over y, x), dp: 8 (over z, core).
Axes of the slice: x: 2, y: 2, z: 4, core: 2. Of those that a mesh axis runs over, the one named last changes fastest.
Arguments:
- tokens: bfloat16 [32, 512, 768], P(('group', 'dp')), may hold values from -6 to 6
- cotangent: bfloat16 [32, 512, 768], P(('group', 'dp')), may hold values from -6 to 6
- replay_count: int32 [1], replicated, may hold values from 8 to 16
- row_length: int32 [32], P(('group', 'dp')), may hold values from 106 to 512, as said below
- response_mask: int32 [32, 512], P(('group', 'dp')), may hold values from 0 to 1, as said below
- proj_weight: bfloat16 [768, 2304], replicated, may hold values from -0.21875 to 0.21875
- query_bias: float32 [768], replicated, may hold values from -3 to 3
- value_bias: float32 [768], replicated, may hold values from -3 to 3
- out_weight: bfloat16 [768, 768], replicated, may hold values from -1.75 to 1.75
- out_bias: float32 [768], replicated, may hold values from -2 to 2
- first_gain: float32 [768], replicated, may hold values from 0.1 to 1.9
- first_shift: float32 [768], replicated, may hold values from -2 to 2
- second_gain: float32 [768], replicated, may hold values from 0.1 to 1.9
- second_shift: float32 [768], replicated, may hold values from -2 to 2
- up_weight: bfloat16 [768, 3072], replicated, may hold values from -0.21875 to 0.21875
- up_bias: float32 [3072], replicated, may hold values from -3 to 3
- down_weight: bfloat16 [3072, 768], replicated, may hold values from -0.109375 to 0.109375
- down_bias: float32 [768], replicated, may hold values from -2 to 2
Outputs:
- output: bfloat16 [32, 512, 768], P(('group', 'dp'))
- tokens_grad: float32 [32, 512, 768], P(('group', 'dp'))
- proj_weight_grad: float32 [768, 2304], P('dp')
- query_bias_grad: float32 [768], P('dp')
- value_bias_grad: float32 [768], P('dp')
- out_weight_grad: float32 [768, 768], P('dp')
- out_bias_grad: float32 [768], P('dp')
- first_gain_grad: float32 [768], P('dp')
- first_shift_grad: float32 [768], P('dp')
- second_gain_grad: float32 [768], P('dp')
- second_shift_grad: float32 [768], P('dp')
- up_weight_grad: float32 [768, 3072], P('dp')
- up_bias_grad: float32 [3072], P('dp')
- down_weight_grad: float32 [3072, 768], P('dp')
- down_bias_grad: float32 [768], P('dp')
The draws below stay inside these ranges and needn't reach their ends.
Inputs may be any that keep to these rules, and one draw needn't show every extreme that they name: `row_length`: positions of a row at or past its length are padding. `response_mask`: zero at positions at or past the row's length; every row has at least one 1.
All inputs are finite; a program needn't handle non-finite values.
Results may differ from the reference program's by a relative error of at most 0.011.
Values sent between devices are 32-bit elements; how exact they have to be, the bound alone decides.
A program may use at most 256 MiB of HBM per device.

```python
import jax
import jax.numpy as jnp
from jax import lax

D = 768
HEAD_DIM = 64
FF = 3072
SEQ = 512
ROWS = 32


def shared_lengths(key):
    row_ids = jnp.arange(ROWS, dtype=jnp.int32)
    lowest = SEQ // 3
    rising = lowest + row_ids * (SEQ - lowest) // max(ROWS - 1, 1)
    jitter = jax.random.randint(jax.random.fold_in(key, 11), (ROWS,), 0, SEQ // 8 + 1)
    lengths = jnp.clip(rising - jitter, 1, SEQ)
    lengths = jnp.where(row_ids == ROWS - 1, SEQ, lengths).astype(jnp.int32)
    prompt = jax.random.randint(jax.random.fold_in(key, 12), (ROWS,), 0, lengths // 2 + 1)
    return (lengths, prompt.astype(jnp.int32))


def draw_row_length(key, part):
    lengths, prompt = shared_lengths(key)
    return lengths


def draw_response_mask(key, part):
    lengths, prompt = shared_lengths(key)
    positions = jnp.arange(SEQ, dtype=jnp.int32)[None, :]
    inside = (positions >= prompt[:, None]) & (positions < lengths[:, None])
    return inside.astype(jnp.int32)


def shard_levels(key, extent, split, least, high):
    loudness = 1.0
    for axis_at, shards_of in split:
        steps = jax.random.uniform(jax.random.fold_in(jax.random.fold_in(key, 6), axis_at), (shards_of,), jnp.float32, least / len(split), high / len(split))
        loudness = loudness * jnp.repeat(jnp.exp(steps), extent[axis_at] // shards_of).reshape((-1,) + (1,) * (len(extent) - 1 - axis_at))
    return loudness


def noise(rng, extent, width, most, cuts=(), kind=jnp.bfloat16):
    array = width * jax.random.normal(rng, extent, jnp.float32)
    if cuts:
        array = array * shard_levels(rng, extent, cuts, -0.22, 0.18)
    return jnp.clip(array, -most, most).astype(kind)


def setup_inputs(seed: int = 0) -> dict:
    splits = jax.random.split(jax.random.key(seed), 19)
    tokens = noise(splits[0], (ROWS, SEQ, D), 1.0, 6.0, ((0, 32),))
    cotangent = noise(splits[1], (ROWS, SEQ, D), 1.0, 6.0, ((0, 32),))
    replay_count = jax.random.randint(splits[2], (1,), ROWS // 4, ROWS // 2 + 1).astype(jnp.int32)
    row_length = draw_row_length(jax.random.fold_in(splits[18], 71), 0)
    response_mask = draw_response_mask(jax.random.fold_in(splits[18], 71), 0)
    proj_weight = noise(splits[5], (D, 3 * D), D ** -0.5, 0.21875)
    query_bias = noise(splits[6], (D,), 0.5, 3.0, (), jnp.float32)
    value_bias = noise(splits[7], (D,), 0.5, 3.0, (), jnp.float32)
    out_weight = noise(splits[8], (D, D), (max(D * 8 // SEQ, 1)) ** -0.5, 1.75)
    out_bias = noise(splits[9], (D,), 0.3, 2.0, (), jnp.float32)
    first_gain = jnp.clip(1.0 + 0.18 * jax.random.normal(splits[10], (D,), jnp.float32), 0.1, 1.9)
    first_shift = noise(splits[11], (D,), 0.3, 2.0, (), jnp.float32)
    second_gain = jnp.clip(1.0 + 0.18 * jax.random.normal(splits[12], (D,), jnp.float32), 0.1, 1.9)
    second_shift = noise(splits[13], (D,), 0.3, 2.0, (), jnp.float32)
    up_weight = noise(splits[14], (D, FF), D ** -0.5, 0.21875)
    up_bias = noise(splits[15], (FF,), 0.5, 3.0, (), jnp.float32)
    down_weight = noise(splits[16], (FF, D), FF ** -0.5, 0.109375)
    down_bias = noise(splits[17], (D,), 0.3, 2.0, (), jnp.float32)
    return {"tokens": tokens, "cotangent": cotangent, "replay_count": replay_count, "row_length": row_length, "response_mask": response_mask, "proj_weight": proj_weight, "query_bias": query_bias, "value_bias": value_bias, "out_weight": out_weight, "out_bias": out_bias, "first_gain": first_gain, "first_shift": first_shift, "second_gain": second_gain, "second_shift": second_shift, "up_weight": up_weight, "up_bias": up_bias, "down_weight": down_weight, "down_bias": down_bias}


@jax.custom_vjp
def low(v):
    return lax.optimization_barrier(v.astype(jnp.bfloat16)).astype(jnp.float32)

@jax.custom_vjp
def low_back(v):
    return v

def low_keep(v):
    return (low(v), None)

def low_pass(kept, grad):
    return (grad,)

def back_keep(v):
    return (v, None)

def back_low(kept, grad):
    return (low(grad),)
low.defvjp(low_keep, low_pass)
low_back.defvjp(back_keep, back_low)
eps_norm = 1e-05
masked_score = -1e+30

def full_product(left, right):
    return jnp.dot(left, right, precision=lax.Precision.HIGHEST, preferred_element_type=jnp.float32)

def layer_norm(inputs, gain, shift):
    average = lax.optimization_barrier(jnp.mean(inputs, axis=-1, keepdims=True))
    centered = inputs - average
    variance = lax.optimization_barrier(jnp.mean(centered * centered, axis=-1, keepdims=True))
    return centered * lax.rsqrt(variance + eps_norm) * gain + shift

def forward(params, row_in, length):
    proj_weight, query_bias, value_bias, out_weight, out_bias, first_gain, first_shift, second_gain, second_shift, up_weight, up_bias, down_weight, down_bias = params
    token_count = row_in.shape[0]
    model_width = out_weight.shape[0]
    head_count = model_width // HEAD_DIM
    score_scale = HEAD_DIM ** (-0.5)
    normed = low(layer_norm(row_in, first_gain, first_shift))
    projected = full_product(normed, proj_weight)
    query_heads = low(low_back(projected[:, :model_width] + query_bias)).reshape(token_count, head_count, HEAD_DIM)
    key_heads = low(low_back(projected[:, model_width:2 * model_width])).reshape(token_count, head_count, HEAD_DIM)
    value_heads = low(low_back(projected[:, 2 * model_width:] + value_bias)).reshape(token_count, head_count, HEAD_DIM)
    scores = jnp.einsum('qhd,khd->hqk', query_heads, key_heads, precision=lax.Precision.HIGHEST) * score_scale
    scores = low_back(scores)
    positions = jnp.arange(token_count)
    allowed = (positions[None, :] <= positions[:, None]) & (positions[None, :] < length)
    scores = jnp.where(allowed[None], scores, masked_score)
    highest = lax.optimization_barrier(jnp.max(scores, axis=-1, keepdims=True))
    raised = jnp.exp(scores - highest)
    prob_table = raised / lax.optimization_barrier(jnp.sum(raised, axis=-1, keepdims=True))
    mixed_heads = jnp.einsum('hqk,khd->qhd', low(prob_table), value_heads, precision=lax.Precision.HIGHEST)
    mixed_flat = low(low_back(mixed_heads.reshape(token_count, model_width)))
    attn_out = low_back(full_product(mixed_flat, out_weight) + out_bias)
    residual = row_in + attn_out
    normed_two = low(layer_norm(residual, second_gain, second_shift))
    hidden = low_back(full_product(normed_two, up_weight) + up_bias)
    activated = low(jax.nn.gelu(hidden, approximate=True))
    branch = low_back(full_product(activated, down_weight) + down_bias)
    return residual + branch

def reference(tokens, cotangent, replay_count, row_length, response_mask, proj_weight, query_bias, value_bias, out_weight, out_bias, first_gain, first_shift, second_gain, second_shift, up_weight, up_bias, down_weight, down_bias):
    params = tuple((weight.astype(jnp.float32) for weight in (proj_weight, query_bias, value_bias, out_weight, out_bias, first_gain, first_shift, second_gain, second_shift, up_weight, up_bias, down_weight, down_bias)))
    row_ids = jnp.arange(ROWS)
    replay_rows = ROWS // 2
    is_replay = row_ids < replay_rows
    in_use = jnp.where(is_replay, row_ids < replay_count[0], True)
    live_tokens = (response_mask * in_use[:, None].astype(jnp.int32)).astype(jnp.float32)
    row_counts = lax.optimization_barrier(jnp.sum(live_tokens, axis=1))
    replay_total = jnp.sum(jnp.where(is_replay, row_counts, 0.0))
    fresh_total = jnp.sum(jnp.where(is_replay, 0.0, row_counts))
    slots = float(replay_rows * SEQ)
    row_scale = jnp.where(is_replay, slots / replay_total, slots / fresh_total)
    token_weight = live_tokens * row_scale[:, None]

    def one_row(running, inputs):
        row_in, row_cot, length, row_weight = inputs

        def local_layer(params_in, layer_in):
            return forward(params_in, layer_in, length)
        result, pullback = jax.vjp(local_layer, params, row_in.astype(jnp.float32))
        param_grads, input_grad = pullback(row_cot.astype(jnp.float32) * row_weight[:, None])
        running = jax.tree.map(jnp.add, running, param_grads)
        return (running, (result.astype(jnp.bfloat16), input_grad))
    zero_grads = jax.tree.map(jnp.zeros_like, params)
    grads, (output, tokens_grad) = lax.scan(one_row, zero_grads, (tokens, cotangent, row_length, token_weight))
    proj_grad, query_grad, value_grad, out_grad, out_bias_grad, first_gain_grad, first_shift_grad, second_gain_grad, second_shift_grad, up_grad, up_bias_grad, down_grad, down_bias_grad = grads
    return (output, tokens_grad, proj_grad, query_grad, value_grad, out_grad, out_bias_grad, first_gain_grad, first_shift_grad, second_gain_grad, second_shift_grad, up_grad, up_bias_grad, down_grad, down_bias_grad)
```

```python
import functools
import math

import jax
import jax.numpy as jnp
from jax import lax
from jax.experimental import pallas as pl
from jax.experimental.pallas import tpu as pltpu
from jax.sharding import PartitionSpec as P

HEAD_DIM = 64
LANES = 128
SUBLANES = 8
MESH = pl.DeviceIdType.MESH


eps_norm = 1e-05
masked_score = -1e30


def layer_norm(inputs, gain, shift):
    average = jnp.mean(inputs, axis=-1, keepdims=True)
    centered = inputs - average
    variance = jnp.mean(centered * centered, axis=-1, keepdims=True)
    return centered * lax.rsqrt(variance + eps_norm) * gain + shift


def tanh_gelu(inputs):
    return jax.nn.gelu(inputs, approximate=True)


def plain_product(left, right):
    return jnp.dot(left, right, preferred_element_type=jnp.float32)


def outer_product(left, right):
    return lax.dot_general(
        left, right, (((0,), (0,)), ((), ())), preferred_element_type=jnp.float32
    )


def transposed_product(left, right):
    return lax.dot_general(
        left, right, (((1,), (1,)), ((), ())), preferred_element_type=jnp.float32
    )


def block_scores(query_block, key_heads, row_start, length, score_scale):
    scores = (
        jnp.einsum("qhd,khd->hqk", query_block, key_heads, preferred_element_type=jnp.float32)
        * score_scale
    )
    query_pos = row_start + jnp.arange(query_block.shape[0])
    key_pos = jnp.arange(key_heads.shape[0])
    allowed = (key_pos[None, :] <= query_pos[:, None]) & (key_pos[None, :] < length)
    return jnp.where(allowed[None], scores, masked_score)


def attend_row(query_heads, key_heads, value_heads, length, block_rows, score_scale):

    def one_block(block_index):
        row_start = block_index * block_rows
        scores = block_scores(query_heads, key_heads, row_start, length, score_scale)
        highest = jnp.max(scores, axis=-1, keepdims=True)
        raised = jnp.exp(scores - highest)
        row_total = jnp.sum(raised, axis=-1, keepdims=True)
        prob_table = raised / row_total
        mixed_block = jnp.einsum(
            "hqk,khd->qhd",
            prob_table.astype(jnp.bfloat16),
            value_heads,
            preferred_element_type=jnp.float32,
        )
        return (mixed_block, highest + jnp.log(row_total))

    block_count = query_heads.shape[0] // block_rows
    mixed_blocks, log_total = lax.map(one_block, jnp.arange(block_count))
    return (mixed_blocks.reshape(query_heads.shape), log_total)


def attend_back(
    query_heads, key_heads, value_heads, length, log_total, mixed_grad, block_rows, score_scale
):

    def one_block(running, inputs):
        key_grad, value_grad = running
        block_index, block_log = inputs
        row_start = block_index * block_rows
        scores = block_scores(query_heads, key_heads, row_start, length, score_scale)
        prob_table = jnp.exp(scores - block_log)
        value_grad = value_grad + jnp.einsum(
            "hqk,qhd->khd",
            prob_table.astype(jnp.bfloat16),
            mixed_grad,
            preferred_element_type=jnp.float32,
        )
        prob_grad = jnp.einsum(
            "qhd,khd->hqk", mixed_grad, value_heads, preferred_element_type=jnp.float32
        )
        inner_sum = jnp.sum(prob_grad * prob_table, axis=-1, keepdims=True)
        score_grad = (prob_table * (prob_grad - inner_sum)).astype(jnp.bfloat16)
        query_grad = (
            jnp.einsum("hqk,khd->qhd", score_grad, key_heads, preferred_element_type=jnp.float32)
            * score_scale
        )
        key_grad = (
            key_grad
            + jnp.einsum(
                "hqk,qhd->khd", score_grad, query_heads, preferred_element_type=jnp.float32
            )
            * score_scale
        )
        return ((key_grad, value_grad), query_grad)

    zero_grads = jnp.zeros(key_heads.shape, jnp.float32)
    block_count = query_heads.shape[0] // block_rows
    (key_grad, value_grad), query_grad = lax.scan(
        one_block, (zero_grads, zero_grads), (jnp.arange(block_count), log_total)
    )
    return (query_grad.reshape(query_heads.shape), key_grad, value_grad)


def plain_shards(
    tokens,
    cotangent,
    replay_count,
    row_length,
    response_mask,
    proj_weight,
    query_bias,
    value_bias,
    out_weight,
    out_bias,
    first_gain,
    first_shift,
    second_gain,
    second_shift,
    up_weight,
    up_bias,
    down_weight,
    down_bias,
):
    group_size = lax.axis_size("group")
    dp_size = lax.axis_size("dp")
    local_rows, token_count, model_width = tokens.shape
    head_count = model_width // HEAD_DIM
    score_scale = HEAD_DIM ** (-0.5)
    block_rows = min(512, token_count)
    head_shape = (local_rows, token_count, head_count, HEAD_DIM)
    first_row = (lax.axis_index("group") * dp_size + lax.axis_index("dp")) * local_rows
    row_ids = first_row + jnp.arange(local_rows)
    replay_rows = local_rows * dp_size * (group_size // 2)
    is_replay = lax.axis_index("group") < group_size // 2
    in_use = jnp.where(is_replay, row_ids < replay_count[0], True)
    live_tokens = (response_mask * in_use[:, None].astype(jnp.int32)).astype(jnp.float32)
    own_total = jnp.sum(live_tokens)
    count_terms = jnp.stack(
        [jnp.where(is_replay, own_total, 0.0), jnp.where(is_replay, 0.0, own_total)]
    )
    totals = lax.psum(count_terms, ("group", "dp"))
    slots = float(replay_rows * token_count)
    row_scale = jnp.where(is_replay, slots / totals[0], slots / totals[1])
    token_weight = live_tokens * row_scale
    flat_in = tokens.reshape(-1, model_width).astype(jnp.float32)
    first_norm, first_back = jax.vjp(layer_norm, flat_in, first_gain, first_shift)
    normed_low = first_norm.astype(jnp.bfloat16)
    projected = plain_product(normed_low, proj_weight)
    query_heads = (projected[:, :model_width] + query_bias).astype(jnp.bfloat16).reshape(head_shape)
    key_heads = projected[:, model_width : 2 * model_width].astype(jnp.bfloat16).reshape(head_shape)
    value_heads = (
        (projected[:, 2 * model_width :] + value_bias).astype(jnp.bfloat16).reshape(head_shape)
    )

    def forward_row(row_inputs):
        query_row, key_row, value_row, length = row_inputs
        return attend_row(query_row, key_row, value_row, length, block_rows, score_scale)

    mixed_heads, log_total = lax.map(forward_row, (query_heads, key_heads, value_heads, row_length))
    mixed_low = mixed_heads.reshape(-1, model_width).astype(jnp.bfloat16)
    attn_out = plain_product(mixed_low, out_weight) + out_bias
    residual = flat_in + attn_out
    second_norm, second_back = jax.vjp(layer_norm, residual, second_gain, second_shift)
    second_low = second_norm.astype(jnp.bfloat16)
    hidden = plain_product(second_low, up_weight) + up_bias
    activated, gelu_back = jax.vjp(tanh_gelu, hidden)
    activated_low = activated.astype(jnp.bfloat16)
    branch = plain_product(activated_low, down_weight) + down_bias
    output = (residual + branch).astype(jnp.bfloat16).reshape(tokens.shape)
    out_grad = cotangent.reshape(-1, model_width).astype(jnp.float32) * token_weight.reshape(-1, 1)
    branch_low = out_grad.astype(jnp.bfloat16)
    down_weight_grad = outer_product(activated_low, branch_low)
    down_bias_grad = jnp.sum(branch_low, axis=0, dtype=jnp.float32)
    activated_grad = transposed_product(branch_low, down_weight)
    (hidden_grad,) = gelu_back(activated_grad)
    hidden_low = hidden_grad.astype(jnp.bfloat16)
    up_weight_grad = outer_product(second_low, hidden_low)
    up_bias_grad = jnp.sum(hidden_low, axis=0, dtype=jnp.float32)
    second_grad = transposed_product(hidden_low, up_weight)
    residual_part, second_gain_grad, second_shift_grad = second_back(second_grad)
    residual_grad = out_grad + residual_part
    attn_low = residual_grad.astype(jnp.bfloat16)
    out_weight_grad = outer_product(mixed_low, attn_low)
    out_bias_grad = jnp.sum(attn_low, axis=0, dtype=jnp.float32)
    mixed_grad = transposed_product(attn_low, out_weight).astype(jnp.bfloat16).reshape(head_shape)

    def backward_row(row_inputs):
        query_row, key_row, value_row, length, row_log, grad_row = row_inputs
        return attend_back(
            query_row, key_row, value_row, length, row_log, grad_row, block_rows, score_scale
        )

    query_grad, key_grad, value_grad = lax.map(
        backward_row, (query_heads, key_heads, value_heads, row_length, log_total, mixed_grad)
    )
    query_low = query_grad.reshape(-1, model_width).astype(jnp.bfloat16)
    key_low = key_grad.reshape(-1, model_width).astype(jnp.bfloat16)
    value_low = value_grad.reshape(-1, model_width).astype(jnp.bfloat16)
    proj_grad_low = jnp.concatenate([query_low, key_low, value_low], axis=1)
    proj_weight_grad = outer_product(normed_low, proj_grad_low)
    query_bias_grad = jnp.sum(query_low, axis=0, dtype=jnp.float32)
    value_bias_grad = jnp.sum(value_low, axis=0, dtype=jnp.float32)
    first_grad = transposed_product(proj_grad_low, proj_weight)
    input_part, first_gain_grad, first_shift_grad = first_back(first_grad)
    tokens_grad = (residual_grad + input_part).reshape(tokens.shape)
    shares = (
        lax.psum_scatter(proj_weight_grad, "dp", scatter_dimension=0, tiled=True),
        lax.psum_scatter(query_bias_grad, "dp", scatter_dimension=0, tiled=True),
        lax.psum_scatter(value_bias_grad, "dp", scatter_dimension=0, tiled=True),
        lax.psum_scatter(out_weight_grad, "dp", scatter_dimension=0, tiled=True),
        lax.psum_scatter(out_bias_grad, "dp", scatter_dimension=0, tiled=True),
        lax.psum_scatter(first_gain_grad, "dp", scatter_dimension=0, tiled=True),
        lax.psum_scatter(first_shift_grad, "dp", scatter_dimension=0, tiled=True),
        lax.psum_scatter(second_gain_grad, "dp", scatter_dimension=0, tiled=True),
        lax.psum_scatter(second_shift_grad, "dp", scatter_dimension=0, tiled=True),
        lax.psum_scatter(up_weight_grad, "dp", scatter_dimension=0, tiled=True),
        lax.psum_scatter(up_bias_grad, "dp", scatter_dimension=0, tiled=True),
        lax.psum_scatter(down_weight_grad, "dp", scatter_dimension=0, tiled=True),
        lax.psum_scatter(down_bias_grad, "dp", scatter_dimension=0, tiled=True),
    )
    summed = lax.psum(tuple(shares), "group")
    pieces = tuple(summed)
    return (output, tokens_grad) + pieces


def bit_of(number, place):
    return lax.rem(lax.div(number, 2**place), 2)


def flip(number, place):
    return number + (1 - 2 * bit_of(number, place)) * 2**place


class Places:
    def __init__(self, group_bits, dp_bits):
        group, spot = lax.axis_index("group"), lax.axis_index("dp")
        core = lax.rem(spot, 2)
        half = group_bits // 2

        def pick(place):
            one, two = (place + half) % group_bits, place % group_bits
            flipped = flip(group, one) + core * (flip(group, two) - flip(group, one))
            side = bit_of(group, one) + core * (bit_of(group, two) - bit_of(group, one))
            return (flipped, spot), side

        self.core = core
        self.partners = [(group, flip(spot, 0))]
        self.sides = [core]
        first, side = pick(0)
        self.partners.append(first)
        self.sides.append(side)
        for place in range(1, dp_bits):
            self.partners.append((group, flip(spot, place)))
            self.sides.append(bit_of(spot, place))
        for place in range(1, group_bits):
            other, side = pick(place)
            self.partners.append(other)
            self.sides.append(side)


class Ring:
    def __init__(self, group_bits, dp_bits, chunks, tiles):
        self.group_bits, self.dp_bits, self.chunks, self.tiles = group_bits, dp_bits, chunks, tiles
        self.blocks = 2 ** (dp_bits - 1)
        self.z_stages = dp_bits - 1
        self.b_stages = group_bits - 1
        self.stages = 2 + self.z_stages + self.b_stages + 1
        self.lags = (2,) * self.stages
        self.after = [0, 0]
        for lag in self.lags[1:-1]:
            self.after.append(self.after[-1] + lag)
        self.order = tuple(range(self.stages - 1, 1, -1))
        self.steps = chunks + self.after[-1]

    def scratch(self):
        half, blocks, lags = self.tiles // 2, self.blocks, self.lags
        tile = (half, SUBLANES, LANES)
        shapes = [(blocks, 2, 2) + tile, (blocks, 2) + tile]
        landing = [(blocks, 2) + tile, (blocks,) + tile]
        left = blocks
        for _ in range(self.z_stages):
            left //= 2
            shapes.append((left, 2) + tile)
            landing.append((left,) + tile)
        shapes += [tile] * self.b_stages
        landing += [tile] * self.b_stages
        send = [pltpu.VMEM((lag,) + shape, jnp.float32) for lag, shape in zip(lags, shapes)]
        recv = [pltpu.VMEM((2 * lag,) + shape, jnp.float32) for lag, shape in zip(lags, landing)]
        send_sems = [pltpu.SemaphoreType.DMA((lag,)) for lag in lags]
        recv_sems = [pltpu.SemaphoreType.DMA((2 * lag,)) for lag in lags]
        return [send, recv, send_sems, recv_sems]

    def bind(self, places, scratch, final):
        self.places = places
        self.send, self.recv, self.send_sems, self.recv_sems = scratch
        self.final = final

    def sending(self, stage, chunk):
        return self.send[stage].at[lax.rem(chunk, self.lags[stage])]

    def half_of(self, stage, ref, side):
        return ref.at[:, side] if stage < 2 + self.z_stages else ref

    def remote(self, source, goal, send_sem, recv_sem, target):
        return pltpu.make_async_remote_copy(
            src_ref=source,
            dst_ref=goal,
            send_sem=send_sem,
            recv_sem=recv_sem,
            device_id=target,
            device_id_type=MESH,
        )

    def copy(self, stage, chunk):
        lag, places = self.lags[stage], self.places
        send_sem = self.send_sems[stage].at[lax.rem(chunk, lag)]
        recv_sem = self.recv_sems[stage].at[lax.rem(chunk, 2 * lag)]
        source = self.half_of(stage, self.sending(stage, chunk), 1 - places.sides[stage])
        goal = self.recv[stage].at[lax.rem(chunk, 2 * lag)]
        return self.remote(source, goal, send_sem, recv_sem, places.partners[stage])

    def gather(self, part):
        half = self.final.at[part, self.places.sides[1]]
        last = self.stages - 1
        return self.remote(half, half, self.send_sems[last].at[0], self.recv_sems[last].at[0], self.places.partners[1])

    def gathered(self):
        return self.gather(slice(None))

    def advance(self, stage, chunk):
        past = stage - 1
        before = self.copy(past, chunk)
        before.wait_recv()
        mine = self.half_of(past, self.sending(past, chunk), self.places.sides[past])
        theirs = self.recv[past].at[lax.rem(chunk, 2 * self.lags[past])]
        last = stage == self.stages - 1
        goal = self.final.at[chunk, self.places.sides[1]] if last else self.sending(stage, chunk)
        goal[...] = (mine[...] + theirs[...]).reshape(goal.shape)
        (self.gather(chunk) if last else self.copy(stage, chunk)).start()
        before.wait_send()

    def pump(self, step, full):
        for stage in self.order:
            chunk = step - self.after[stage]
            if full:
                self.advance(stage, chunk)
                continue

            @pl.when((chunk >= 0) & (chunk < self.chunks))
            def _():
                self.advance(stage, chunk)


def contract_rows(left, right):
    return lax.dot_general(left, right, (((0,), (0,)), ((), ())), preferred_element_type=jnp.float32)


SLAB = 512
PAIR = 2 * HEAD_DIM
ROWS_AT_ONCE = 128
NARROW = ("query", "value", "out", "gain1", "shift1", "gain2", "shift2", "down")


def slab(index, width):
    return pl.ds(pl.multiple_of(index * width, width), width)


def moments(rows):
    centered = rows - jnp.mean(rows, axis=-1, keepdims=True)
    variance = jnp.mean(centered * centered, axis=-1, keepdims=True)
    return centered, lax.rsqrt(variance + eps_norm)


def gelu_and_slope(inputs):
    root = math.sqrt(2.0 / math.pi)
    square = inputs * inputs
    bent = jnp.tanh(root * (inputs + 0.044715 * (square * inputs)))
    rise = 0.5 + 0.5 * bent
    slope = rise + (0.5 * root) * inputs * (1.0 - bent * bent) * (1.0 + 3 * 0.044715 * square)
    return inputs * rise, slope


def norm_back(grad_rows, centered, rstd, gain):
    hat = centered * rstd
    gained = grad_rows * gain
    inner = jnp.mean(gained * hat, axis=-1, keepdims=True)
    back = (gained - jnp.mean(gained, axis=-1, keepdims=True) - hat * inner) * rstd
    sums = (jnp.sum(grad_rows * hat, axis=0, keepdims=True), jnp.sum(grad_rows, axis=0, keepdims=True))
    return back, sums


def layer_kernel(ring, slots, dp_size, *refs):
    (
        tokens_ref, cotangent_hbm, replay_ref, length_ref, mask_ref, proj_hbm, query_bias_ref, value_bias_ref, out_hbm,
        out_bias_ref, gain1_ref, shift1_ref, gain2_ref, shift2_ref, up_hbm, up_bias_ref, down_hbm, down_bias_ref,
        low_ref, grad_ref, final_ref, bias_ref,
        proj_ref, out_ref, up_ref, down_ref, norm1_ref, heads_ref, mixed_ref, residual_ref, norm2_ref, act_ref,
        hidden_ref, branch_ref, weight_ref, sum_ref, attn_ref, mixed_grad_ref, heads_grad_ref, log_ref,
        mixed_turned_ref, turned_ref, pad_ref, key_sum_ref, value_sum_ref, cotangent_ref, load_sems, small_send, small_recv, small_sems, wide_send, wide_recv, wide_sems, *scratch
    ) = refs
    f32, bf16 = jnp.float32, jnp.bfloat16
    token_count, width = tokens_ref.shape
    half_scale = HEAD_DIM ** (-0.5)
    places = Places(ring.group_bits, ring.dp_bits)
    turns = len(places.partners)
    stages = ring.stages
    sems = scratch[2 * stages - 2 :]
    ring.bind(
        places,
        (scratch[: stages - 1], scratch[stages - 1 : 2 * stages - 2], sems[:stages], sems[stages:]),
        final_ref,
    )

    loads = [
        pltpu.make_async_copy(source, goal, load_sems.at[place])
        for place, (source, goal) in enumerate(
            (
                (proj_hbm, proj_ref),
                (out_hbm, out_ref),
                (up_hbm, up_ref),
                (down_hbm, down_ref),
                (cotangent_hbm, cotangent_ref),
            )
        )
    ]
    for load in loads:
        load.start()

    barrier = pltpu.get_barrier_semaphore()
    for partner in places.partners:
        pl.semaphore_signal(barrier, inc=1, device_id=partner, device_id_type=MESH)

    def exchange(buffers, landing, sems, turn):
        return pltpu.make_async_remote_copy(
            src_ref=buffers.at[turn],
            dst_ref=landing.at[turn],
            send_sem=sems.at[0, turn],
            recv_sem=sems.at[1, turn],
            device_id=places.partners[turn],
            device_id_type=MESH,
        )

    small = functools.partial(exchange, small_send, small_recv, small_sems)
    wide = functools.partial(exchange, wide_send, wide_recv, wide_sems)

    group_half = 2**ring.group_bits // 2
    group = lax.axis_index("group")
    row = group * dp_size + lax.axis_index("dp")
    row_blocks = [slice(at, at + ROWS_AT_ONCE) for at in range(0, token_count, ROWS_AT_ONCE)]
    for rows in row_blocks:
        centered, rstd = moments(tokens_ref[rows, :].astype(f32))
        norm1_ref[rows, :] = (centered * rstd * gain1_ref[...] + shift1_ref[...]).astype(bf16)

    used = jnp.where((group >= group_half) | (row < replay_ref[0]), 1.0, 0.0)
    live = mask_ref[...].astype(f32) * used
    side = lax.div(group, group_half)
    tile_rows = lax.broadcasted_iota(jnp.int32, (SUBLANES, LANES), 0)
    small_send[0] = jnp.where(tile_rows == side, jnp.sum(live, axis=1, keepdims=True), 0.0)
    loads[0].wait()
    for third, bias in enumerate((query_bias_ref, None, value_bias_ref)):

        columns = slice(third * width, (third + 1) * width)
        product = plain_product(norm1_ref[...], proj_ref[:, columns])
        if bias is not None:
            product = product + bias[...]
        heads_ref[:, columns] = product.astype(bf16)

    pl.semaphore_wait(barrier, turns)

    length = length_ref[0]
    lanes = lax.broadcasted_iota(jnp.int32, (1, PAIR), 1)
    own_lanes = (lanes < HEAD_DIM, lanes >= HEAD_DIM)
    spare_lanes = (lanes == HEAD_DIM, lanes == 0)
    block = token_count // 2
    blocks = ((0, block), (block, token_count))
    causal = lax.broadcasted_iota(jnp.int32, (block, block), 0) <= lax.broadcasted_iota(jnp.int32, (block, block), 1)
    padding = lax.broadcasted_iota(jnp.int32, (token_count, PAIR), 0) >= length
    for head in range(2):
        pad_ref[head] = jnp.where(padding & spare_lanes[head], masked_score, 0.0).astype(bf16)

    def pair_columns(third, pair):
        return pl.ds(pl.multiple_of(third * width + pair * PAIR, PAIR), PAIR)

    def only(head, array):
        return jnp.where(own_lanes[head], array, jnp.zeros_like(array))

    def head_scores(head, key, query, start, keys):
        padded = jnp.where(own_lanes[head], key[:keys], pad_ref[head, :keys])
        one = jnp.where(spare_lanes[head], 1.0, 0.0).astype(bf16)
        asking = jnp.where(own_lanes[head], query[start : start + block] * half_scale, one)
        scores = transposed_product(padded, asking)
        last = jnp.where(causal, scores[start:], masked_score)
        return last if start == 0 else jnp.concatenate([scores[:start], last], axis=0)

    def attend(pair):
        query = heads_ref[:, pair_columns(0, pair)]
        key = heads_ref[:, pair_columns(1, pair)]
        turned = heads_ref[:, pair_columns(2, pair)].T
        for start, keys in blocks:
            mixed = []
            for head in range(2):
                scores = head_scores(head, key, query, start, keys)
                highest = jnp.max(scores, axis=0, keepdims=True)
                raised = jnp.exp(scores - highest)
                total = jnp.sum(raised, axis=0, keepdims=True)
                log_ref[pair, head : head + 1, start : start + block] = highest + jnp.log(total)
                product = plain_product(turned[head * HEAD_DIM : (head + 1) * HEAD_DIM, :keys], raised.astype(bf16))
                mixed.append(product * (1.0 / total))
            low = jnp.concatenate(mixed, axis=0).astype(bf16)
            mixed_turned_ref[slab(pair, PAIR), start : start + block] = low
            mixed_ref[start : start + block, slab(pair, PAIR)] = low.T

    def count_turn(turn):
        if turn:
            small(turn - 1).wait()
            small_send[turn] = small_send[turn - 1] + small_recv[turn - 1]
        if turn < turns:
            small(turn).start()

    count_turn(0)

    @pl.loop(0, width // (2 * PAIR))
    def _(at):
        attend(2 * at)
        attend(2 * at + 1)
        for turn in range(1, 4):

            @pl.when(at + 1 == turn)
            def _():
                count_turn(turn)


    loads[1].wait()

    product = plain_product(mixed_ref[...], out_ref[...]) + out_bias_ref[...]
    residual_ref[...] = tokens_ref[...].astype(f32) + product
    count_turn(4)

    for rows in row_blocks:
        centered, rstd = moments(residual_ref[rows, :])
        low = (centered * rstd * gain2_ref[...] + shift2_ref[...]).astype(bf16)
        norm2_ref[rows, :] = low
        turned_ref[:, rows] = low.T

    for turn in range(5, turns + 1):
        count_turn(turn)
    loads[4].wait()

    totals = jnp.sum(jnp.where(tile_rows == side, small_send[turns], 0.0), axis=0, keepdims=True)
    weight_ref[...] = jnp.broadcast_to(live, (LANES, token_count)).T * (slots / totals)

    def out_grad(rows):
        pieces = [
            cotangent_ref[rows, at * LANES : (at + 1) * LANES].astype(f32) * weight_ref[rows, :]
            for at in range(width // LANES)
        ]
        return jnp.concatenate(pieces, axis=1)

    def keep_narrow(name, vector):
        place = NARROW.index(name)
        for at in range(width // LANES):
            wide_send[0, at * SUBLANES + place : at * SUBLANES + place + 1, :] = vector[:, at * LANES : (at + 1) * LANES]

    def row_sums(body, count):
        zeros = tuple(jnp.zeros((1, width), f32) for _ in range(count))

        def one(at, sums):
            return tuple(old + new for old, new in zip(sums, body(slab(at, ROWS_AT_ONCE))))

        return lax.fori_loop(0, token_count // ROWS_AT_ONCE, one, zeros)

    def branch_rows(rows):
        low = out_grad(rows).astype(bf16)
        branch_ref[rows, :] = low
        return jnp.sum(low.astype(f32), axis=0, keepdims=True)

    keep_narrow("down", sum(branch_rows(rows) for rows in row_blocks))

    goal = ring.send[0]
    halves, blocks_of = ring.tiles // 2, ring.blocks

    def put(column, product):
        rows = product.shape[0] // (2 * blocks_of * SUBLANES)
        shaped = product.reshape(blocks_of, 2, rows, SUBLANES, LANES)
        for part in range(rows // halves):
            place = column * (rows // halves) + part
            goal[place // 2, :, :, place % 2] = shaped[:, :, part * halves : (part + 1) * halves]

    def put_all(product):
        for column in range(SLAB // LANES):
            put(column, product[:, column * LANES : (column + 1) * LANES])

    def one_step(step, make, work, more, full=True):
        first = 2 * step
        make()
        ring.copy(0, first).start()
        ring.copy(0, first + 1).start()
        work()
        ring.pump(first, full)
        ring.advance(1, first)
        more()
        ring.pump(first + 1, full)
        ring.advance(1, first + 1)

    loads[2].wait()
    loads[3].wait()
    slabs = up_ref.shape[1] // SLAB
    narrow_rows = width // LANES * SUBLANES

    def hidden_slab(at, size=SLAB):
        columns = slab(at, size)
        hidden = plain_product(norm2_ref[...], up_ref[:, columns]) + up_bias_ref[columns]
        act, slope = gelu_and_slope(hidden)
        act_ref[columns, :] = act.astype(bf16).T
        low = (transposed_product(branch_ref[...], down_ref[columns, :]) * slope).astype(bf16)
        hidden_ref[:, columns] = low
        bias_sum = jnp.sum(low.astype(f32), axis=0, keepdims=True)
        for part in range(size // LANES):
            place = narrow_rows + at * (size // LANES) + part
            wide_send[0, pl.ds(place, 1), :] = bias_sum[:, part * LANES : (part + 1) * LANES]

    for part in range(2):
        hidden_slab(part, SLAB // 2)
        columns = slice(part * SLAB // 2, (part + 1) * SLAB // 2)
        product = plain_product(turned_ref[...], hidden_ref[:, columns])
        for column in range(2):
            put(2 * part + column, product[:, column * LANES : (column + 1) * LANES])
        ring.copy(0, part).start()
    ring.advance(1, 0)
    grad_ref[...] = transposed_product(hidden_ref[:, :SLAB], up_ref[:, :SLAB])
    ring.advance(1, 1)
    hidden_slab(1)

    @pl.loop(1, slabs)
    def _(step):
        columns = slab(step, SLAB)

        def make():
            put_all(plain_product(turned_ref[...], hidden_ref[:, columns]))

        def work():
            @pl.when(step + 1 < slabs)
            def _():
                hidden_slab(step + 1)

        def more():
            grad_ref[...] += transposed_product(hidden_ref[:, columns], up_ref[:, columns])

        one_step(step, make, work, more, full=False)

    def second_back(rows):
        residual = residual_ref[rows, :]
        turned_ref[:, rows] = norm1_ref[rows, :].T
        centered, rstd = moments(residual)
        back, sums = norm_back(grad_ref[rows, :], centered, rstd, gain2_ref[...])
        residual_grad = out_grad(rows) + back
        grad_ref[rows, :] = residual_grad
        low = residual_grad.astype(bf16)
        attn_ref[rows, :] = low
        return sums + (jnp.sum(low.astype(f32), axis=0, keepdims=True),)

    def pair_back(pair, part):
        start, keys = blocks[part]
        here = slice(start, start + block)
        query = heads_ref[:, pair_columns(0, pair)]
        key = heads_ref[:, pair_columns(1, pair)]
        value = heads_ref[:, pair_columns(2, pair)]
        grad = mixed_grad_ref[here, slab(pair, PAIR)]
        key_turned = key[:keys].T
        query_grads, key_grad, value_grad = [], 0.0, 0.0
        for head in range(2):
            scores = head_scores(head, key, query, start, keys)
            probs = jnp.exp(scores - log_ref[pair, head : head + 1, here])
            value_grad += plain_product(probs.astype(bf16), only(head, grad))
            prob_grad = transposed_product(only(head, value[:keys]), grad)
            inner = jnp.sum(prob_grad * probs, axis=0, keepdims=True)
            low = (probs * (prob_grad - inner)).astype(bf16)
            query_grads.append(plain_product(key_turned[head * HEAD_DIM : (head + 1) * HEAD_DIM], low))
            key_grad += plain_product(low, only(head, query[here]))
        query_low = (jnp.concatenate(query_grads, axis=0) * half_scale).astype(bf16).T
        heads_grad_ref[here, pair_columns(0, pair)] = query_low
        keep_pair("query", pair, part, query_low)
        if part == 0:
            key_sum_ref[...] = key_grad
            value_sum_ref[...] = value_grad
            return
        for third, total, factor, earlier in (
            (1, key_grad, half_scale, key_sum_ref),
            (2, value_grad, 1.0, value_sum_ref),
        ):
            first = ((total[:block] + earlier[...]) * factor).astype(bf16)
            second = (total[block:] * factor).astype(bf16)
            heads_grad_ref[:block, pair_columns(third, pair)] = first
            heads_grad_ref[block:, pair_columns(third, pair)] = second
            if third == 2:
                keep_pair("value", pair, 0, first)
                keep_pair("value", pair, 1, second)

    def keep_pair(name, pair, part, low):
        place = pl.ds(pair * SUBLANES + NARROW.index(name), 1)
        total = jnp.sum(low.astype(f32), axis=0, keepdims=True)
        wide_send[0, place, :] = total + wide_send[0, place, :] if part else total

    def make_down(step):
        pair, part = lax.div(step - slabs, 2), lax.rem(step - slabs, 2)
        rows = act_ref.shape[0] // (2 * blocks_of)
        starts = [pl.multiple_of(place * rows + part * (rows // 2), 2 * SUBLANES) for place in range(2 * blocks_of)]
        tall = jnp.concatenate([act_ref[pl.ds(start, rows // 2), :] for start in starts], axis=0)
        product = plain_product(tall, branch_ref[:, slab(pair, 2 * LANES)])
        for column in range(2):
            put(column, product[:, column * LANES : (column + 1) * LANES])

    def second_norm():
        for name, vector in zip(("gain2", "shift2", "out"), row_sums(second_back, 3)):
            keep_narrow(name, vector)

    def mixed_back():
        mixed_grad_ref[...] = transposed_product(attn_ref[...], out_ref[...]).astype(bf16)

    one_step(slabs, functools.partial(make_down, slabs), second_norm, mixed_back)

    @pl.loop(slabs + 1, 2 * slabs)
    def _(step):
        pair = step - slabs - 1
        one_step(
            step,
            functools.partial(make_down, step),
            functools.partial(pair_back, pair, 0),
            functools.partial(pair_back, pair, 1),
        )

    def make_out():
        put_all(plain_product(mixed_turned_ref[...], attn_ref[:, :SLAB]))

    step = 2 * slabs
    pair = slabs - 1
    one_step(step, make_out, functools.partial(pair_back, pair, 0), functools.partial(pair_back, pair, 1))

    rest = width - SLAB

    def make_both():
        part = plain_product(mixed_turned_ref[...], attn_ref[:, SLAB:])
        more = plain_product(turned_ref[...], heads_grad_ref[:, : SLAB - rest])
        for column in range(rest // LANES):
            put(column, part[:, column * LANES : (column + 1) * LANES])
        for column in range((SLAB - rest) // LANES):
            put(column + rest // LANES, more[:, column * LANES : (column + 1) * LANES])

    def norm1_grads():
        sum_ref[...] = transposed_product(heads_grad_ref[...], proj_ref[...])

    def first_back(rows):
        centered, rstd = moments(tokens_ref[rows, :].astype(f32))
        back, sums = norm_back(sum_ref[rows, :], centered, rstd, gain1_ref[...])
        grad_ref[rows, :] += back
        return sums

    def first_norm():
        for name, vector in zip(("gain1", "shift1"), row_sums(first_back, 2)):
            keep_narrow(name, vector)
        wide(0).start()

    step += 1
    one_step(step, make_both, norm1_grads, first_norm)
    step += 1

    def add_branch(at):
        columns = slab(at, SLAB)
        residual_ref[...] += contract_rows(act_ref[columns, :], down_ref[columns, :])

    def wide_turn(now, first):
        for turn in range(turns):

            @pl.when(now == first + turn)
            def _():
                wide(turn).wait()
                wide_send[turn + 1] = wide_send[turn] + wide_recv[turn]
                if turn + 1 < turns:
                    wide(turn + 1).start()

    last_steps = 3 * slabs - step

    @pl.loop(step, 3 * slabs)
    def _(now):
        def make():
            start = pl.multiple_of((now - step) * SLAB + SLAB - rest, LANES)
            put_all(plain_product(turned_ref[...], heads_grad_ref[:, pl.ds(start, SLAB)]))

        def work():
            wide_turn(now, step)

            @pl.when(now - step < slabs // 2)
            def _():
                add_branch(now - step)

        def more():
            @pl.when(now - step < slabs // 2)
            def _():
                add_branch(now - step + slabs // 2)

        one_step(now, make, work, more)

    @pl.loop(ring.chunks, ring.steps)
    def _(now):
        ring.pump(now, False)
        wide_turn(now, ring.chunks - last_steps)

        @pl.when(now == ring.chunks)
        def _():
            low_ref[...] = (residual_ref[...] + down_bias_ref[...]).astype(bf16)

    ring.gathered().wait()
    bias_ref[...] = wide_send[turns]


def layer(group_size, dp_size, slots, arrays):
    f32, bf16 = jnp.float32, jnp.bfloat16
    group_bits, dp_bits = int(math.log2(group_size)), int(math.log2(dp_size))
    token_count, width = arrays[0].shape
    hidden = arrays[14].shape[1]
    ring = Ring(group_bits, dp_bits, 6 * hidden // SLAB, hidden // dp_size // SUBLANES // 2)
    turns = group_bits + dp_bits
    send, recv, send_sems, recv_sems = ring.scratch()
    tile = (SUBLANES, LANES)
    wide = ((len(NARROW) * width + hidden) // LANES, LANES)
    vmem, anywhere = pl.BlockSpec(memory_space=pltpu.VMEM), pl.BlockSpec(memory_space=pl.ANY)
    in_specs = [vmem] * len(arrays)
    for place in (1, 5, 8, 14, 16):
        in_specs[place] = anywhere
    for place in (2, 3):
        in_specs[place] = pl.BlockSpec(memory_space=pltpu.SMEM)
    return pl.pallas_call(
        functools.partial(layer_kernel, ring, slots, dp_size),
        out_shape=(
            pltpu.VMEM((token_count, width), bf16),
            pltpu.VMEM((token_count, width), f32),
            pltpu.VMEM((ring.chunks, 2, ring.tiles // 2) + tile, f32),
            pltpu.VMEM(wide, f32),
        ),
        in_specs=in_specs,
        out_specs=(vmem,) * 4,
        scratch_shapes=[
            pltpu.VMEM((width, 3 * width), bf16),
            pltpu.VMEM((width, width), bf16),
            pltpu.VMEM((width, hidden), bf16),
            pltpu.VMEM((hidden, width), bf16),
            pltpu.VMEM((token_count, width), bf16),
            pltpu.VMEM((token_count, 3 * width), bf16),
            pltpu.VMEM((token_count, width), bf16),
            pltpu.VMEM((token_count, width), f32),
            pltpu.VMEM((token_count, width), bf16),
            pltpu.VMEM((hidden, token_count), bf16),
            pltpu.VMEM((token_count, hidden), bf16),
            pltpu.VMEM((token_count, width), bf16),
            pltpu.VMEM((token_count, LANES), f32),
            pltpu.VMEM((token_count, width), f32),
            pltpu.VMEM((token_count, width), bf16),
            pltpu.VMEM((token_count, width), bf16),
            pltpu.VMEM((token_count, 3 * width), bf16),
            pltpu.VMEM((width // PAIR, 2, token_count), f32),
            pltpu.VMEM((width, token_count), bf16),
            pltpu.VMEM((width, token_count), bf16),
            pltpu.VMEM((2, token_count, PAIR), bf16),
            pltpu.VMEM((token_count // 2, PAIR), f32),
            pltpu.VMEM((token_count // 2, PAIR), f32),
            pltpu.VMEM((token_count, width), bf16),
            pltpu.SemaphoreType.DMA((5,)),
            pltpu.VMEM((turns + 1,) + tile, f32),
            pltpu.VMEM((turns,) + tile, f32),
            pltpu.SemaphoreType.DMA((2, turns)),
            pltpu.VMEM((turns + 1,) + wide, f32),
            pltpu.VMEM((turns,) + wide, f32),
            pltpu.SemaphoreType.DMA((2, turns)),
        ]
        + send
        + recv
        + send_sems
        + recv_sems,
        compiler_params=pltpu.CompilerParams(
            collective_id=0, has_side_effects=True, vmem_limit_bytes=54 * 2**20
        ),
    )(*arrays)


def place_kernel(*refs):
    low_ref, grad_ref, tiles_ref, bias_ref = refs[:4]
    goals = refs[4:19]
    proj_ref, out_ref, up_ref, down_ref = refs[19:23]
    narrow_refs, up_bias_ref, store_sems = refs[23:31], refs[31], refs[32]
    chunks, _, half = tiles_ref.shape[:3]
    third = chunks // 3
    sources = (low_ref, grad_ref, proj_ref, out_ref, up_ref, down_ref) + narrow_refs + (up_bias_ref,)
    stores = [pltpu.make_async_copy(*pair, store_sems.at[place]) for place, pair in enumerate(zip(sources, goals))]
    for store in stores[:2]:
        store.start()
    rows = proj_ref.shape[0]
    width = out_ref.shape[2]
    out_columns = width // LANES
    spot = lax.axis_index("dp")
    piece = rows * SUBLANES
    columns = width // LANES
    vectors = jnp.concatenate(
        [bias_ref[at * SUBLANES : (at + 1) * SUBLANES, :] for at in range(columns)], axis=1
    )
    vectors = pltpu.roll(vectors, lax.rem(width - spot * piece, width), 1)
    for place, ref in enumerate(narrow_refs):
        ref[...] = vectors[place, :piece]
    count = up_bias_ref.shape[0] // LANES
    for at in range(count):
        row = columns * SUBLANES + spot * count + at
        up_bias_ref[at * LANES : (at + 1) * LANES] = bias_ref[pl.ds(row, 1), :].reshape(LANES)
    for store in stores[6:]:
        store.start()
    parts = down_ref.shape[0] // half
    for place in range(2 * third):
        pair, inside = divmod(place, 2 * parts)
        part, column = divmod(inside, parts)
        part, column = 2 * part + column % 2, 2 * pair + column // 2
        goal = down_ref.at[part * half : (part + 1) * half, :, column * LANES : (column + 1) * LANES]
        goal[...] = tiles_ref[third + place // 2, place % 2]
    stores[5].start()
    for kind in (0, 2):
        for column in range(third * 2 * (half // rows)):
            place, part = divmod(column, half // rows)
            goal, at = up_ref, column
            if kind == 2:
                goal, at = (out_ref, column) if column < out_columns else (proj_ref, column - out_columns)
            source = tiles_ref[kind * third + place // 2, place % 2, part * rows : (part + 1) * rows]
            goal[:, :, at * LANES : (at + 1) * LANES] = source
        for store in stores[2:4] if kind else stores[4:5]:
            store.start()
    for store in stores:
        store.wait()


def place_results(dp_size, hidden, output, tokens_grad, final, bias):
    f32 = jnp.float32
    width = output.shape[1]
    rows = width // dp_size
    tile_rows = rows // SUBLANES
    shape = jax.ShapeDtypeStruct
    anywhere, vmem = pl.BlockSpec(memory_space=pl.ANY), pl.BlockSpec(memory_space=pltpu.VMEM)
    large = (
        (output.shape, output.dtype),
        (tokens_grad.shape, f32),
        ((tile_rows, SUBLANES, 3 * width), f32),
        ((tile_rows, SUBLANES, width), f32),
        ((tile_rows, SUBLANES, hidden), f32),
        ((hidden // dp_size // SUBLANES, SUBLANES, width), f32),
    )
    vectors = (((rows,), f32),) * len(NARROW) + (((hidden // dp_size,), f32),)
    return pl.pallas_call(
        place_kernel,
        out_shape=tuple(shape(*one) for one in large + vectors),
        in_specs=[vmem] * 4,
        out_specs=(anywhere,) * len(large + vectors),
        scratch_shapes=[pltpu.VMEM(*one) for one in large[2:] + vectors]
        + [pltpu.SemaphoreType.DMA((len(large + vectors),))],
        compiler_params=pltpu.CompilerParams(vmem_limit_bytes=16 * 2**20),
    )(output, tokens_grad, final, bias)


def ring_shards(*arrays):
    group_size, dp_size = lax.axis_size("group"), lax.axis_size("dp")
    tokens = arrays[0]
    _, token_count, width = tokens.shape
    hidden = arrays[14].shape[1]
    slots = float(dp_size * (group_size // 2) * token_count)
    flat = [tokens[0], arrays[1][0], *arrays[2:]]
    placed = place_results(dp_size, hidden, *layer(group_size, dp_size, slots, flat))
    output, tokens_grad, proj, out, up, down = placed[:6]
    narrow = dict(zip(NARROW, placed[6:14]))
    rows = width // dp_size
    return (
        output[None],
        tokens_grad[None],
        proj.reshape(rows, 3 * width),
        narrow["query"],
        narrow["value"],
        out.reshape(rows, width),
        narrow["out"],
        narrow["gain1"],
        narrow["shift1"],
        narrow["gain2"],
        narrow["shift2"],
        up.reshape(rows, hidden),
        placed[14],
        down.reshape(hidden // dp_size, width),
        narrow["down"],
    )


def solution(mesh):
    in_specs = (
        P(("group", "dp"), None, None),
        P(("group", "dp"), None, None),
        P(),
        P(("group", "dp")),
        P(("group", "dp"), None),
        P(),
        P(),
        P(),
        P(),
        P(),
        P(),
        P(),
        P(),
        P(),
        P(),
        P(),
        P(),
        P(),
    )
    out_specs = (
        P(("group", "dp"), None, None),
        P(("group", "dp"), None, None),
        P("dp", None),
        P("dp"),
        P("dp"),
        P("dp", None),
        P("dp"),
        P("dp"),
        P("dp"),
        P("dp"),
        P("dp"),
        P("dp", None),
        P("dp"),
        P("dp", None),
        P("dp"),
    )
    group_size, dp_size = mesh.shape["group"], mesh.shape["dp"]

    def body(*arrays):
        tokens, out_weight, up_weight = arrays[0], arrays[8], arrays[14]
        whole_tiles = (out_weight.shape[0] // dp_size) % SUBLANES == 0
        one_row = tokens.shape[:2] == (1, 512) and up_weight.shape == (768, 3072)
        powers = group_size == 4 and dp_size >= 4 and dp_size & (dp_size - 1) == 0
        return (ring_shards if whole_tiles and one_row and powers else plain_shards)(*arrays)

    return jax.shard_map(body, mesh=mesh, in_specs=in_specs, out_specs=out_specs, check_vma=False)
```

```python
import functools
import math

import jax
import jax.numpy as jnp
from jax import lax
from jax.experimental import pallas as pl
from jax.experimental.pallas import tpu as pltpu
from jax.sharding import PartitionSpec as P

HEAD_DIM = 64
LANES = 128
SUBLANES = 8
MESH = pl.DeviceIdType.MESH


eps_norm = 1e-05
masked_score = -1e30


def layer_norm(inputs, gain, shift):
    average = jnp.mean(inputs, axis=-1, keepdims=True)
    centered = inputs - average
    variance = jnp.mean(centered * centered, axis=-1, keepdims=True)
    return centered * lax.rsqrt(variance + eps_norm) * gain + shift


def tanh_gelu(inputs):
    return jax.nn.gelu(inputs, approximate=True)


def plain_product(left, right):
    return jnp.dot(left, right, preferred_element_type=jnp.float32)


def outer_product(left, right):
    return lax.dot_general(
        left, right, (((0,), (0,)), ((), ())), preferred_element_type=jnp.float32
    )


def transposed_product(left, right):
    return lax.dot_general(
        left, right, (((1,), (1,)), ((), ())), preferred_element_type=jnp.float32
    )


def block_scores(query_block, key_heads, row_start, length, score_scale):
    scores = (
        jnp.einsum("qhd,khd->hqk", query_block, key_heads, preferred_element_type=jnp.float32)
        * score_scale
    )
    query_pos = row_start + jnp.arange(query_block.shape[0])
    key_pos = jnp.arange(key_heads.shape[0])
    allowed = (key_pos[None, :] <= query_pos[:, None]) & (key_pos[None, :] < length)
    return jnp.where(allowed[None], scores, masked_score)


def attend_row(query_heads, key_heads, value_heads, length, block_rows, score_scale):

    def one_block(block_index):
        row_start = block_index * block_rows
        scores = block_scores(query_heads, key_heads, row_start, length, score_scale)
        highest = jnp.max(scores, axis=-1, keepdims=True)
        raised = jnp.exp(scores - highest)
        row_total = jnp.sum(raised, axis=-1, keepdims=True)
        prob_table = raised / row_total
        mixed_block = jnp.einsum(
            "hqk,khd->qhd",
            prob_table.astype(jnp.bfloat16),
            value_heads,
            preferred_element_type=jnp.float32,
        )
        return (mixed_block, highest + jnp.log(row_total))

    block_count = query_heads.shape[0] // block_rows
    mixed_blocks, log_total = lax.map(one_block, jnp.arange(block_count))
    return (mixed_blocks.reshape(query_heads.shape), log_total)


def attend_back(
    query_heads, key_heads, value_heads, length, log_total, mixed_grad, block_rows, score_scale
):

    def one_block(running, inputs):
        key_grad, value_grad = running
        block_index, block_log = inputs
        row_start = block_index * block_rows
        scores = block_scores(query_heads, key_heads, row_start, length, score_scale)
        prob_table = jnp.exp(scores - block_log)
        value_grad = value_grad + jnp.einsum(
            "hqk,qhd->khd",
            prob_table.astype(jnp.bfloat16),
            mixed_grad,
            preferred_element_type=jnp.float32,
        )
        prob_grad = jnp.einsum(
            "qhd,khd->hqk", mixed_grad, value_heads, preferred_element_type=jnp.float32
        )
        inner_sum = jnp.sum(prob_grad * prob_table, axis=-1, keepdims=True)
        score_grad = (prob_table * (prob_grad - inner_sum)).astype(jnp.bfloat16)
        query_grad = (
            jnp.einsum("hqk,khd->qhd", score_grad, key_heads, preferred_element_type=jnp.float32)
            * score_scale
        )
        key_grad = (
            key_grad
            + jnp.einsum(
                "hqk,qhd->khd", score_grad, query_heads, preferred_element_type=jnp.float32
            )
            * score_scale
        )
        return ((key_grad, value_grad), query_grad)

    zero_grads = jnp.zeros(key_heads.shape, jnp.float32)
    block_count = query_heads.shape[0] // block_rows
    (key_grad, value_grad), query_grad = lax.scan(
        one_block, (zero_grads, zero_grads), (jnp.arange(block_count), log_total)
    )
    return (query_grad.reshape(query_heads.shape), key_grad, value_grad)


def plain_shards(
    tokens,
    cotangent,
    replay_count,
    row_length,
    response_mask,
    proj_weight,
    query_bias,
    value_bias,
    out_weight,
    out_bias,
    first_gain,
    first_shift,
    second_gain,
    second_shift,
    up_weight,
    up_bias,
    down_weight,
    down_bias,
):
    group_size = lax.axis_size("group")
    dp_size = lax.axis_size("dp")
    local_rows, token_count, model_width = tokens.shape
    head_count = model_width // HEAD_DIM
    score_scale = HEAD_DIM ** (-0.5)
    block_rows = min(512, token_count)
    head_shape = (local_rows, token_count, head_count, HEAD_DIM)
    first_row = (lax.axis_index("group") * dp_size + lax.axis_index("dp")) * local_rows
    row_ids = first_row + jnp.arange(local_rows)
    replay_rows = local_rows * dp_size * (group_size // 2)
    is_replay = lax.axis_index("group") < group_size // 2
    in_use = jnp.where(is_replay, row_ids < replay_count[0], True)
    live_tokens = (response_mask * in_use[:, None].astype(jnp.int32)).astype(jnp.float32)
    own_total = jnp.sum(live_tokens)
    count_terms = jnp.stack(
        [jnp.where(is_replay, own_total, 0.0), jnp.where(is_replay, 0.0, own_total)]
    )
    totals = lax.psum(count_terms, ("group", "dp"))
    slots = float(replay_rows * token_count)
    row_scale = jnp.where(is_replay, slots / totals[0], slots / totals[1])
    token_weight = live_tokens * row_scale
    flat_in = tokens.reshape(-1, model_width).astype(jnp.float32)
    first_norm, first_back = jax.vjp(layer_norm, flat_in, first_gain, first_shift)
    normed_low = first_norm.astype(jnp.bfloat16)
    projected = plain_product(normed_low, proj_weight)
    query_heads = (projected[:, :model_width] + query_bias).astype(jnp.bfloat16).reshape(head_shape)
    key_heads = projected[:, model_width : 2 * model_width].astype(jnp.bfloat16).reshape(head_shape)
    value_heads = (
        (projected[:, 2 * model_width :] + value_bias).astype(jnp.bfloat16).reshape(head_shape)
    )

    def forward_row(row_inputs):
        query_row, key_row, value_row, length = row_inputs
        return attend_row(query_row, key_row, value_row, length, block_rows, score_scale)

    mixed_heads, log_total = lax.map(forward_row, (query_heads, key_heads, value_heads, row_length))
    mixed_low = mixed_heads.reshape(-1, model_width).astype(jnp.bfloat16)
    attn_out = plain_product(mixed_low, out_weight) + out_bias
    residual = flat_in + attn_out
    second_norm, second_back = jax.vjp(layer_norm, residual, second_gain, second_shift)
    second_low = second_norm.astype(jnp.bfloat16)
    hidden = plain_product(second_low, up_weight) + up_bias
    activated, gelu_back = jax.vjp(tanh_gelu, hidden)
    activated_low = activated.astype(jnp.bfloat16)
    branch = plain_product(activated_low, down_weight) + down_bias
    output = (residual + branch).astype(jnp.bfloat16).reshape(tokens.shape)
    out_grad = cotangent.reshape(-1, model_width).astype(jnp.float32) * token_weight.reshape(-1, 1)
    branch_low = out_grad.astype(jnp.bfloat16)
    down_weight_grad = outer_product(activated_low, branch_low)
    down_bias_grad = jnp.sum(branch_low, axis=0, dtype=jnp.float32)
    activated_grad = transposed_product(branch_low, down_weight)
    (hidden_grad,) = gelu_back(activated_grad)
    hidden_low = hidden_grad.astype(jnp.bfloat16)
    up_weight_grad = outer_product(second_low, hidden_low)
    up_bias_grad = jnp.sum(hidden_low, axis=0, dtype=jnp.float32)
    second_grad = transposed_product(hidden_low, up_weight)
    residual_part, second_gain_grad, second_shift_grad = second_back(second_grad)
    residual_grad = out_grad + residual_part
    attn_low = residual_grad.astype(jnp.bfloat16)
    out_weight_grad = outer_product(mixed_low, attn_low)
    out_bias_grad = jnp.sum(attn_low, axis=0, dtype=jnp.float32)
    mixed_grad = transposed_product(attn_low, out_weight).astype(jnp.bfloat16).reshape(head_shape)

    def backward_row(row_inputs):
        query_row, key_row, value_row, length, row_log, grad_row = row_inputs
        return attend_back(
            query_row, key_row, value_row, length, row_log, grad_row, block_rows, score_scale
        )

    query_grad, key_grad, value_grad = lax.map(
        backward_row, (query_heads, key_heads, value_heads, row_length, log_total, mixed_grad)
    )
    query_low = query_grad.reshape(-1, model_width).astype(jnp.bfloat16)
    key_low = key_grad.reshape(-1, model_width).astype(jnp.bfloat16)
    value_low = value_grad.reshape(-1, model_width).astype(jnp.bfloat16)
    proj_grad_low = jnp.concatenate([query_low, key_low, value_low], axis=1)
    proj_weight_grad = outer_product(normed_low, proj_grad_low)
    query_bias_grad = jnp.sum(query_low, axis=0, dtype=jnp.float32)
    value_bias_grad = jnp.sum(value_low, axis=0, dtype=jnp.float32)
    first_grad = transposed_product(proj_grad_low, proj_weight)
    input_part, first_gain_grad, first_shift_grad = first_back(first_grad)
    tokens_grad = (residual_grad + input_part).reshape(tokens.shape)
    shares = (
        lax.psum_scatter(proj_weight_grad, "dp", scatter_dimension=0, tiled=True),
        lax.psum_scatter(query_bias_grad, "dp", scatter_dimension=0, tiled=True),
        lax.psum_scatter(value_bias_grad, "dp", scatter_dimension=0, tiled=True),
        lax.psum_scatter(out_weight_grad, "dp", scatter_dimension=0, tiled=True),
        lax.psum_scatter(out_bias_grad, "dp", scatter_dimension=0, tiled=True),
        lax.psum_scatter(first_gain_grad, "dp", scatter_dimension=0, tiled=True),
        lax.psum_scatter(first_shift_grad, "dp", scatter_dimension=0, tiled=True),
        lax.psum_scatter(second_gain_grad, "dp", scatter_dimension=0, tiled=True),
        lax.psum_scatter(second_shift_grad, "dp", scatter_dimension=0, tiled=True),
        lax.psum_scatter(up_weight_grad, "dp", scatter_dimension=0, tiled=True),
        lax.psum_scatter(up_bias_grad, "dp", scatter_dimension=0, tiled=True),
        lax.psum_scatter(down_weight_grad, "dp", scatter_dimension=0, tiled=True),
        lax.psum_scatter(down_bias_grad, "dp", scatter_dimension=0, tiled=True),
    )
    summed = lax.psum(tuple(shares), "group")
    pieces = tuple(summed)
    return (output, tokens_grad) + pieces


def bit_of(number, place):
    return lax.rem(lax.div(number, 2**place), 2)


def flip(number, place):
    return number + (1 - 2 * bit_of(number, place)) * 2**place


class Places:
    def __init__(self, group_bits, dp_bits):
        group, spot = lax.axis_index("group"), lax.axis_index("dp")
        core = lax.rem(spot, 2)
        half = group_bits // 2

        def pick(place):
            one, two = (place + half) % group_bits, place % group_bits
            flipped = flip(group, one) + core * (flip(group, two) - flip(group, one))
            side = bit_of(group, one) + core * (bit_of(group, two) - bit_of(group, one))
            return (flipped, spot), side

        self.core = core
        self.partners = [(group, flip(spot, 0))]
        self.sides = [core]
        first, side = pick(0)
        self.partners.append(first)
        self.sides.append(side)
        for place in range(1, dp_bits):
            self.partners.append((group, flip(spot, place)))
            self.sides.append(bit_of(spot, place))
        for place in range(1, group_bits):
            other, side = pick(place)
            self.partners.append(other)
            self.sides.append(side)


class Ring:
    def __init__(self, group_bits, dp_bits, chunks, tiles):
        self.group_bits, self.dp_bits, self.chunks, self.tiles = group_bits, dp_bits, chunks, tiles
        self.blocks = 2 ** (dp_bits - 1)
        self.z_stages = dp_bits - 1
        self.b_stages = group_bits - 1
        self.stages = 2 + self.z_stages + self.b_stages + 1
        self.lags = (2,) * self.stages
        self.after = [0, 0]
        for lag in self.lags[1:-1]:
            self.after.append(self.after[-1] + lag)
        self.order = tuple(range(self.stages - 1, 1, -1))
        self.steps = chunks + self.after[-1]

    def scratch(self):
        half, blocks, lags = self.tiles // 2, self.blocks, self.lags
        tile = (half, SUBLANES, LANES)
        shapes = [(blocks, 2, 2) + tile, (blocks, 2) + tile]
        landing = [(blocks, 2) + tile, (blocks,) + tile]
        left = blocks
        for _ in range(self.z_stages):
            left //= 2
            shapes.append((left, 2) + tile)
            landing.append((left,) + tile)
        shapes += [tile] * self.b_stages
        landing += [tile] * self.b_stages
        send = [pltpu.VMEM((lag,) + shape, jnp.float32) for lag, shape in zip(lags, shapes)]
        recv = [pltpu.VMEM((2 * lag,) + shape, jnp.float32) for lag, shape in zip(lags, landing)]
        send_sems = [pltpu.SemaphoreType.DMA((lag,)) for lag in lags]
        recv_sems = [pltpu.SemaphoreType.DMA((2 * lag,)) for lag in lags]
        return [send, recv, send_sems, recv_sems]

    def bind(self, places, scratch, final):
        self.places = places
        self.send, self.recv, self.send_sems, self.recv_sems = scratch
        self.final = final

    def sending(self, stage, chunk):
        return self.send[stage].at[lax.rem(chunk, self.lags[stage])]

    def half_of(self, stage, ref, side):
        return ref.at[:, side] if stage < 2 + self.z_stages else ref

    def remote(self, source, goal, send_sem, recv_sem, target):
        return pltpu.make_async_remote_copy(
            src_ref=source,
            dst_ref=goal,
            send_sem=send_sem,
            recv_sem=recv_sem,
            device_id=target,
            device_id_type=MESH,
        )

    def copy(self, stage, chunk):
        lag, places = self.lags[stage], self.places
        send_sem = self.send_sems[stage].at[lax.rem(chunk, lag)]
        recv_sem = self.recv_sems[stage].at[lax.rem(chunk, 2 * lag)]
        source = self.half_of(stage, self.sending(stage, chunk), 1 - places.sides[stage])
        goal = self.recv[stage].at[lax.rem(chunk, 2 * lag)]
        return self.remote(source, goal, send_sem, recv_sem, places.partners[stage])

    def gather(self, part):
        half = self.final.at[part, self.places.sides[1]]
        last = self.stages - 1
        return self.remote(half, half, self.send_sems[last].at[0], self.recv_sems[last].at[0], self.places.partners[1])

    def gathered(self):
        return self.gather(slice(None))

    def advance(self, stage, chunk):
        past = stage - 1
        before = self.copy(past, chunk)
        before.wait_recv()
        mine = self.half_of(past, self.sending(past, chunk), self.places.sides[past])
        theirs = self.recv[past].at[lax.rem(chunk, 2 * self.lags[past])]
        last = stage == self.stages - 1
        goal = self.final.at[chunk, self.places.sides[1]] if last else self.sending(stage, chunk)
        goal[...] = (mine[...] + theirs[...]).reshape(goal.shape)
        (self.gather(chunk) if last else self.copy(stage, chunk)).start()
        before.wait_send()

    def pump(self, step, full):
        for stage in self.order:
            chunk = step - self.after[stage]
            if full:
                self.advance(stage, chunk)
                continue

            @pl.when((chunk >= 0) & (chunk < self.chunks))
            def _():
                self.advance(stage, chunk)


def contract_rows(left, right):
    return lax.dot_general(left, right, (((0,), (0,)), ((), ())), preferred_element_type=jnp.float32)


SLAB = 512
PAIR = 2 * HEAD_DIM
ROWS_AT_ONCE = 128
NARROW = ("query", "value", "out", "gain1", "shift1", "gain2", "shift2", "down")


def slab(index, width):
    return pl.ds(pl.multiple_of(index * width, width), width)


def moments(rows):
    centered = rows - jnp.mean(rows, axis=-1, keepdims=True)
    variance = jnp.mean(centered * centered, axis=-1, keepdims=True)
    return centered, lax.rsqrt(variance + eps_norm)


def gelu_and_slope(inputs):
    root = math.sqrt(2.0 / math.pi)
    square = inputs * inputs
    bent = jnp.tanh(root * (inputs + 0.044715 * (square * inputs)))
    rise = 0.5 + 0.5 * bent
    slope = rise + (0.5 * root) * inputs * (1.0 - bent * bent) * (1.0 + 3 * 0.044715 * square)
    return inputs * rise, slope


def norm_back(grad_rows, centered, rstd, gain):
    hat = centered * rstd
    gained = grad_rows * gain
    inner = jnp.mean(gained * hat, axis=-1, keepdims=True)
    back = (gained - jnp.mean(gained, axis=-1, keepdims=True) - hat * inner) * rstd
    sums = (jnp.sum(grad_rows * hat, axis=0, keepdims=True), jnp.sum(grad_rows, axis=0, keepdims=True))
    return back, sums


def layer_kernel(ring, slots, dp_size, *refs):
    (
        tokens_ref, cotangent_hbm, replay_ref, length_ref, mask_ref, proj_hbm, query_bias_ref, value_bias_ref, out_hbm,
        out_bias_ref, gain1_ref, shift1_ref, gain2_ref, shift2_ref, up_hbm, up_bias_ref, down_hbm, down_bias_ref,
        low_ref, grad_ref, final_ref, bias_ref,
        proj_ref, out_ref, up_ref, down_ref, norm1_ref, heads_ref, mixed_ref, residual_ref, norm2_ref, act_ref,
        hidden_ref, branch_ref, weight_ref, sum_ref, attn_ref, mixed_grad_ref, heads_grad_ref, log_ref,
        mixed_turned_ref, turned_ref, pad_ref, key_sum_ref, value_sum_ref, cotangent_ref, load_sems, small_send, small_recv, small_sems, wide_send, wide_recv, wide_sems, *scratch
    ) = refs
    f32, bf16 = jnp.float32, jnp.bfloat16
    token_count, width = tokens_ref.shape
    half_scale = HEAD_DIM ** (-0.5)
    places = Places(ring.group_bits, ring.dp_bits)
    turns = len(places.partners)
    stages = ring.stages
    sems = scratch[2 * stages - 2 :]
    ring.bind(
        places,
        (scratch[: stages - 1], scratch[stages - 1 : 2 * stages - 2], sems[:stages], sems[stages:]),
        final_ref,
    )

    loads = [
        pltpu.make_async_copy(source, goal, load_sems.at[place])
        for place, (source, goal) in enumerate(
            (
                (proj_hbm, proj_ref),
                (out_hbm, out_ref),
                (up_hbm, up_ref),
                (down_hbm, down_ref),
                (cotangent_hbm, cotangent_ref),
            )
        )
    ]
    for load in loads:
        load.start()

    barrier = pltpu.get_barrier_semaphore()
    for partner in places.partners:
        pl.semaphore_signal(barrier, inc=1, device_id=partner, device_id_type=MESH)

    def exchange(buffers, landing, sems, turn):
        return pltpu.make_async_remote_copy(
            src_ref=buffers.at[turn],
            dst_ref=landing.at[turn],
            send_sem=sems.at[0, turn],
            recv_sem=sems.at[1, turn],
            device_id=places.partners[turn],
            device_id_type=MESH,
        )

    small = functools.partial(exchange, small_send, small_recv, small_sems)
    wide = functools.partial(exchange, wide_send, wide_recv, wide_sems)

    group_half = 2**ring.group_bits // 2
    group = lax.axis_index("group")
    row = group * dp_size + lax.axis_index("dp")
    row_blocks = [slice(at, at + ROWS_AT_ONCE) for at in range(0, token_count, ROWS_AT_ONCE)]
    used = jnp.where((group >= group_half) | (row < replay_ref[0]), 1.0, 0.0)
    live = mask_ref[...].astype(f32) * used
    side = lax.div(group, group_half)
    tile_rows = lax.broadcasted_iota(jnp.int32, (SUBLANES, LANES), 0)
    small_send[0] = jnp.where(tile_rows == side, jnp.sum(live, axis=1, keepdims=True), 0.0)
    loads[0].wait()
    row_halves = [row_blocks[: len(row_blocks) // 2], row_blocks[len(row_blocks) // 2 :]]
    for row_half in row_halves:
        for rows in row_half:
            centered, rstd = moments(tokens_ref[rows, :].astype(f32))
            norm1_ref[rows, :] = (centered * rstd * gain1_ref[...] + shift1_ref[...]).astype(bf16)
        half = slice(row_half[0].start, row_half[-1].stop)
        for third, bias in enumerate((query_bias_ref, None, value_bias_ref)):
            columns = slice(third * width, (third + 1) * width)
            product = plain_product(norm1_ref[half, :], proj_ref[:, columns])
            if bias is not None:
                product = product + bias[...]
            heads_ref[half, columns] = product.astype(bf16)

    pl.semaphore_wait(barrier, turns)

    length = length_ref[0]
    lanes = lax.broadcasted_iota(jnp.int32, (1, PAIR), 1)
    own_lanes = (lanes < HEAD_DIM, lanes >= HEAD_DIM)
    spare_lanes = (lanes == HEAD_DIM, lanes == 0)
    block = token_count // 2
    blocks = ((0, block), (block, token_count))
    causal = lax.broadcasted_iota(jnp.int32, (block, block), 0) <= lax.broadcasted_iota(jnp.int32, (block, block), 1)
    padding = lax.broadcasted_iota(jnp.int32, (token_count, PAIR), 0) >= length
    for head in range(2):
        pad_ref[head] = jnp.where(padding & spare_lanes[head], masked_score, 0.0).astype(bf16)

    def pair_columns(third, pair):
        return pl.ds(pl.multiple_of(third * width + pair * PAIR, PAIR), PAIR)

    def only(head, array):
        return jnp.where(own_lanes[head], array, jnp.zeros_like(array))

    def head_scores(head, key, query, start, keys):
        padded = jnp.where(own_lanes[head], key[:keys], pad_ref[head, :keys])
        one = jnp.where(spare_lanes[head], 1.0, 0.0).astype(bf16)
        asking = jnp.where(own_lanes[head], query[start : start + block] * half_scale, one)
        scores = transposed_product(padded, asking)
        last = jnp.where(causal, scores[start:], masked_score)
        return last if start == 0 else jnp.concatenate([scores[:start], last], axis=0)

    def attend(pair):
        query = heads_ref[:, pair_columns(0, pair)]
        key = heads_ref[:, pair_columns(1, pair)]
        turned = heads_ref[:, pair_columns(2, pair)].T
        for start, keys in blocks:
            mixed = []
            for head in range(2):
                scores = head_scores(head, key, query, start, keys)
                highest = jnp.max(scores, axis=0, keepdims=True)
                raised = jnp.exp(scores - highest)
                total = jnp.sum(raised, axis=0, keepdims=True)
                log_ref[pair, head : head + 1, start : start + block] = highest + jnp.log(total)
                product = plain_product(turned[head * HEAD_DIM : (head + 1) * HEAD_DIM, :keys], raised.astype(bf16))
                mixed.append(product * (1.0 / total))
            low = jnp.concatenate(mixed, axis=0).astype(bf16)
            mixed_turned_ref[slab(pair, PAIR), start : start + block] = low
            mixed_ref[start : start + block, slab(pair, PAIR)] = low.T

    def count_turn(turn):
        if turn:
            small(turn - 1).wait()
            small_send[turn] = small_send[turn - 1] + small_recv[turn - 1]
        if turn < turns:
            small(turn).start()

    count_turn(0)

    @pl.loop(0, width // (2 * PAIR))
    def _(at):
        attend(2 * at)
        attend(2 * at + 1)
        for turn in range(1, 4):

            @pl.when(at + 1 == turn)
            def _():
                count_turn(turn)


    loads[1].wait()

    for row_half in row_halves:
        half = slice(row_half[0].start, row_half[-1].stop)
        product = plain_product(mixed_ref[half, :], out_ref[...]) + out_bias_ref[...]
        residual_ref[half, :] = tokens_ref[half, :].astype(f32) + product
        for rows in row_half:
            centered, rstd = moments(residual_ref[rows, :])
            low = (centered * rstd * gain2_ref[...] + shift2_ref[...]).astype(bf16)
            norm2_ref[rows, :] = low
            turned_ref[:, rows] = low.T
    count_turn(4)

    for turn in range(5, turns + 1):
        count_turn(turn)
    loads[4].wait()

    totals = jnp.sum(jnp.where(tile_rows == side, small_send[turns], 0.0), axis=0, keepdims=True)
    weight_ref[...] = jnp.broadcast_to(live, (LANES, token_count)).T * (slots / totals)

    def out_grad(rows):
        pieces = [
            cotangent_ref[rows, at * LANES : (at + 1) * LANES].astype(f32) * weight_ref[rows, :]
            for at in range(width // LANES)
        ]
        return jnp.concatenate(pieces, axis=1)

    def keep_narrow(name, vector):
        place = NARROW.index(name)
        for at in range(width // LANES):
            wide_send[0, at * SUBLANES + place : at * SUBLANES + place + 1, :] = vector[:, at * LANES : (at + 1) * LANES]

    def row_sums(body, count):
        zeros = tuple(jnp.zeros((1, width), f32) for _ in range(count))

        def one(at, sums):
            return tuple(old + new for old, new in zip(sums, body(slab(at, ROWS_AT_ONCE))))

        return lax.fori_loop(0, token_count // ROWS_AT_ONCE, one, zeros)

    def branch_rows(rows):
        low = out_grad(rows).astype(bf16)
        branch_ref[rows, :] = low
        return jnp.sum(low.astype(f32), axis=0, keepdims=True)

    keep_narrow("down", sum(branch_rows(rows) for rows in row_blocks))

    goal = ring.send[0]
    halves, blocks_of = ring.tiles // 2, ring.blocks

    def put(column, product):
        rows = product.shape[0] // (2 * blocks_of * SUBLANES)
        shaped = product.reshape(blocks_of, 2, rows, SUBLANES, LANES)
        for part in range(rows // halves):
            place = column * (rows // halves) + part
            goal[place // 2, :, :, place % 2] = shaped[:, :, part * halves : (part + 1) * halves]

    def put_all(product):
        for column in range(SLAB // LANES):
            put(column, product[:, column * LANES : (column + 1) * LANES])

    def one_step(step, make, work, more, full=True):
        first = 2 * step
        make()
        ring.copy(0, first).start()
        ring.copy(0, first + 1).start()
        work()
        ring.pump(first, full)
        ring.advance(1, first)
        more()
        ring.pump(first + 1, full)
        ring.advance(1, first + 1)

    loads[2].wait()
    loads[3].wait()
    slabs = up_ref.shape[1] // SLAB
    narrow_rows = width // LANES * SUBLANES

    def hidden_slab(at, size=SLAB):
        columns = slab(at, size)
        hidden = plain_product(norm2_ref[...], up_ref[:, columns]) + up_bias_ref[columns]
        act, slope = gelu_and_slope(hidden)
        act_ref[columns, :] = act.astype(bf16).T
        low = (transposed_product(branch_ref[...], down_ref[columns, :]) * slope).astype(bf16)
        hidden_ref[:, columns] = low
        bias_sum = jnp.sum(low.astype(f32), axis=0, keepdims=True)
        for part in range(size // LANES):
            place = narrow_rows + at * (size // LANES) + part
            wide_send[0, pl.ds(place, 1), :] = bias_sum[:, part * LANES : (part + 1) * LANES]

    for part in range(2):
        hidden_slab(part, SLAB // 2)
        columns = slice(part * SLAB // 2, (part + 1) * SLAB // 2)
        product = plain_product(turned_ref[...], hidden_ref[:, columns])
        for column in range(2):
            put(2 * part + column, product[:, column * LANES : (column + 1) * LANES])
        ring.copy(0, part).start()
    ring.advance(1, 0)
    grad_ref[...] = transposed_product(hidden_ref[:, :SLAB], up_ref[:, :SLAB])
    ring.advance(1, 1)
    hidden_slab(1)

    @pl.loop(1, slabs)
    def _(step):
        columns = slab(step, SLAB)

        def make():
            put_all(plain_product(turned_ref[...], hidden_ref[:, columns]))

        def work():
            @pl.when(step + 1 < slabs)
            def _():
                hidden_slab(step + 1)

        def more():
            grad_ref[...] += transposed_product(hidden_ref[:, columns], up_ref[:, columns])

        one_step(step, make, work, more, full=False)

    def second_back(rows):
        residual = residual_ref[rows, :]
        turned_ref[:, rows] = norm1_ref[rows, :].T
        centered, rstd = moments(residual)
        back, sums = norm_back(grad_ref[rows, :], centered, rstd, gain2_ref[...])
        residual_grad = out_grad(rows) + back
        grad_ref[rows, :] = residual_grad
        low = residual_grad.astype(bf16)
        attn_ref[rows, :] = low
        return sums + (jnp.sum(low.astype(f32), axis=0, keepdims=True),)

    def pair_back(pair, part):
        start, keys = blocks[part]
        here = slice(start, start + block)
        query = heads_ref[:, pair_columns(0, pair)]
        key = heads_ref[:, pair_columns(1, pair)]
        value = heads_ref[:, pair_columns(2, pair)]
        grad = mixed_grad_ref[here, slab(pair, PAIR)]
        key_turned = key[:keys].T
        query_grads, key_grad, value_grad = [], 0.0, 0.0
        for head in range(2):
            scores = head_scores(head, key, query, start, keys)
            probs = jnp.exp(scores - log_ref[pair, head : head + 1, here])
            value_grad += plain_product(probs.astype(bf16), only(head, grad))
            prob_grad = transposed_product(only(head, value[:keys]), grad)
            inner = jnp.sum(prob_grad * probs, axis=0, keepdims=True)
            low = (probs * (prob_grad - inner)).astype(bf16)
            query_grads.append(plain_product(key_turned[head * HEAD_DIM : (head + 1) * HEAD_DIM], low))
            key_grad += plain_product(low, only(head, query[here]))
        query_low = (jnp.concatenate(query_grads, axis=0) * half_scale).astype(bf16).T
        heads_grad_ref[here, pair_columns(0, pair)] = query_low
        keep_pair("query", pair, part, query_low)
        if part == 0:
            key_sum_ref[...] = key_grad
            value_sum_ref[...] = value_grad
            return
        for third, total, factor, earlier in (
            (1, key_grad, half_scale, key_sum_ref),
            (2, value_grad, 1.0, value_sum_ref),
        ):
            first = ((total[:block] + earlier[...]) * factor).astype(bf16)
            second = (total[block:] * factor).astype(bf16)
            heads_grad_ref[:block, pair_columns(third, pair)] = first
            heads_grad_ref[block:, pair_columns(third, pair)] = second
            if third == 2:
                keep_pair("value", pair, 0, first)
                keep_pair("value", pair, 1, second)

    def keep_pair(name, pair, part, low):
        place = pl.ds(pair * SUBLANES + NARROW.index(name), 1)
        total = jnp.sum(low.astype(f32), axis=0, keepdims=True)
        wide_send[0, place, :] = total + wide_send[0, place, :] if part else total

    def make_down(step):
        pair, part = lax.div(step - slabs, 2), lax.rem(step - slabs, 2)
        rows = act_ref.shape[0] // (2 * blocks_of)
        starts = [pl.multiple_of(place * rows + part * (rows // 2), 2 * SUBLANES) for place in range(2 * blocks_of)]
        tall = jnp.concatenate([act_ref[pl.ds(start, rows // 2), :] for start in starts], axis=0)
        product = plain_product(tall, branch_ref[:, slab(pair, 2 * LANES)])
        for column in range(2):
            put(column, product[:, column * LANES : (column + 1) * LANES])

    def second_norm():
        for name, vector in zip(("gain2", "shift2", "out"), row_sums(second_back, 3)):
            keep_narrow(name, vector)

    def mixed_back():
        mixed_grad_ref[...] = transposed_product(attn_ref[...], out_ref[...]).astype(bf16)

    one_step(slabs, functools.partial(make_down, slabs), second_norm, mixed_back)

    @pl.loop(slabs + 1, 2 * slabs)
    def _(step):
        pair = step - slabs - 1
        one_step(
            step,
            functools.partial(make_down, step),
            functools.partial(pair_back, pair, 0),
            functools.partial(pair_back, pair, 1),
        )

    def make_out():
        put_all(plain_product(mixed_turned_ref[...], attn_ref[:, :SLAB]))

    step = 2 * slabs
    pair = slabs - 1
    one_step(step, make_out, functools.partial(pair_back, pair, 0), functools.partial(pair_back, pair, 1))

    rest = width - SLAB

    def make_both():
        part = plain_product(mixed_turned_ref[...], attn_ref[:, SLAB:])
        more = plain_product(turned_ref[...], heads_grad_ref[:, : SLAB - rest])
        for column in range(rest // LANES):
            put(column, part[:, column * LANES : (column + 1) * LANES])
        for column in range((SLAB - rest) // LANES):
            put(column + rest // LANES, more[:, column * LANES : (column + 1) * LANES])

    def norm1_grads():
        sum_ref[...] = transposed_product(heads_grad_ref[...], proj_ref[...])

    def first_back(rows):
        centered, rstd = moments(tokens_ref[rows, :].astype(f32))
        back, sums = norm_back(sum_ref[rows, :], centered, rstd, gain1_ref[...])
        grad_ref[rows, :] += back
        return sums

    def first_norm():
        for name, vector in zip(("gain1", "shift1"), row_sums(first_back, 2)):
            keep_narrow(name, vector)
        wide(0).start()

    step += 1
    one_step(step, make_both, norm1_grads, first_norm)
    step += 1

    def add_branch(at):
        columns = slab(at, SLAB)
        residual_ref[...] += contract_rows(act_ref[columns, :], down_ref[columns, :])

    def wide_turn(now, first):
        for turn in range(turns):

            @pl.when(now == first + turn)
            def _():
                wide(turn).wait()
                wide_send[turn + 1] = wide_send[turn] + wide_recv[turn]
                if turn + 1 < turns:
                    wide(turn + 1).start()

    last_steps = 3 * slabs - step

    @pl.loop(step, 3 * slabs)
    def _(now):
        def make():
            start = pl.multiple_of((now - step) * SLAB + SLAB - rest, LANES)
            put_all(plain_product(turned_ref[...], heads_grad_ref[:, pl.ds(start, SLAB)]))

        def work():
            wide_turn(now, step)

            @pl.when(now - step < slabs // 2)
            def _():
                add_branch(now - step)

        def more():
            @pl.when(now - step < slabs // 2)
            def _():
                add_branch(now - step + slabs // 2)

        one_step(now, make, work, more)

    @pl.loop(ring.chunks, ring.steps)
    def _(now):
        ring.pump(now, False)
        wide_turn(now, ring.chunks - last_steps)

        @pl.when(now == ring.chunks)
        def _():
            low_ref[...] = (residual_ref[...] + down_bias_ref[...]).astype(bf16)

    ring.gathered().wait()
    bias_ref[...] = wide_send[turns]


def layer(group_size, dp_size, slots, arrays):
    f32, bf16 = jnp.float32, jnp.bfloat16
    group_bits, dp_bits = int(math.log2(group_size)), int(math.log2(dp_size))
    token_count, width = arrays[0].shape
    hidden = arrays[14].shape[1]
    ring = Ring(group_bits, dp_bits, 6 * hidden // SLAB, hidden // dp_size // SUBLANES // 2)
    turns = group_bits + dp_bits
    send, recv, send_sems, recv_sems = ring.scratch()
    tile = (SUBLANES, LANES)
    wide = ((len(NARROW) * width + hidden) // LANES, LANES)
    vmem, anywhere = pl.BlockSpec(memory_space=pltpu.VMEM), pl.BlockSpec(memory_space=pl.ANY)
    in_specs = [vmem] * len(arrays)
    for place in (1, 5, 8, 14, 16):
        in_specs[place] = anywhere
    for place in (2, 3):
        in_specs[place] = pl.BlockSpec(memory_space=pltpu.SMEM)
    return pl.pallas_call(
        functools.partial(layer_kernel, ring, slots, dp_size),
        out_shape=(
            pltpu.VMEM((token_count, width), bf16),
            pltpu.VMEM((token_count, width), f32),
            pltpu.VMEM((ring.chunks, 2, ring.tiles // 2) + tile, f32),
            pltpu.VMEM(wide, f32),
        ),
        in_specs=in_specs,
        out_specs=(vmem,) * 4,
        scratch_shapes=[
            pltpu.VMEM((width, 3 * width), bf16),
            pltpu.VMEM((width, width), bf16),
            pltpu.VMEM((width, hidden), bf16),
            pltpu.VMEM((hidden, width), bf16),
            pltpu.VMEM((token_count, width), bf16),
            pltpu.VMEM((token_count, 3 * width), bf16),
            pltpu.VMEM((token_count, width), bf16),
            pltpu.VMEM((token_count, width), f32),
            pltpu.VMEM((token_count, width), bf16),
            pltpu.VMEM((hidden, token_count), bf16),
            pltpu.VMEM((token_count, hidden), bf16),
            pltpu.VMEM((token_count, width), bf16),
            pltpu.VMEM((token_count, LANES), f32),
            pltpu.VMEM((token_count, width), f32),
            pltpu.VMEM((token_count, width), bf16),
            pltpu.VMEM((token_count, width), bf16),
            pltpu.VMEM((token_count, 3 * width), bf16),
            pltpu.VMEM((width // PAIR, 2, token_count), f32),
            pltpu.VMEM((width, token_count), bf16),
            pltpu.VMEM((width, token_count), bf16),
            pltpu.VMEM((2, token_count, PAIR), bf16),
            pltpu.VMEM((token_count // 2, PAIR), f32),
            pltpu.VMEM((token_count // 2, PAIR), f32),
            pltpu.VMEM((token_count, width), bf16),
            pltpu.SemaphoreType.DMA((5,)),
            pltpu.VMEM((turns + 1,) + tile, f32),
            pltpu.VMEM((turns,) + tile, f32),
            pltpu.SemaphoreType.DMA((2, turns)),
            pltpu.VMEM((turns + 1,) + wide, f32),
            pltpu.VMEM((turns,) + wide, f32),
            pltpu.SemaphoreType.DMA((2, turns)),
        ]
        + send
        + recv
        + send_sems
        + recv_sems,
        compiler_params=pltpu.CompilerParams(
            collective_id=0, has_side_effects=True, vmem_limit_bytes=54 * 2**20
        ),
    )(*arrays)


def place_kernel(*refs):
    low_ref, grad_ref, tiles_ref, bias_ref = refs[:4]
    goals = refs[4:19]
    proj_ref, out_ref, up_ref, down_ref = refs[19:23]
    narrow_refs, up_bias_ref, store_sems = refs[23:31], refs[31], refs[32]
    chunks, _, half = tiles_ref.shape[:3]
    third = chunks // 3
    sources = (low_ref, grad_ref, proj_ref, out_ref, up_ref, down_ref) + narrow_refs + (up_bias_ref,)
    stores = [pltpu.make_async_copy(*pair, store_sems.at[place]) for place, pair in enumerate(zip(sources, goals))]
    for store in stores[:2]:
        store.start()
    rows = proj_ref.shape[0]
    width = out_ref.shape[2]
    out_columns = width // LANES
    spot = lax.axis_index("dp")
    piece = rows * SUBLANES
    columns = width // LANES
    vectors = jnp.concatenate(
        [bias_ref[at * SUBLANES : (at + 1) * SUBLANES, :] for at in range(columns)], axis=1
    )
    vectors = pltpu.roll(vectors, lax.rem(width - spot * piece, width), 1)
    for place, ref in enumerate(narrow_refs):
        ref[...] = vectors[place, :piece]
    count = up_bias_ref.shape[0] // LANES
    for at in range(count):
        row = columns * SUBLANES + spot * count + at
        up_bias_ref[at * LANES : (at + 1) * LANES] = bias_ref[pl.ds(row, 1), :].reshape(LANES)
    for store in stores[6:]:
        store.start()
    parts = down_ref.shape[0] // half
    for place in range(2 * third):
        pair, inside = divmod(place, 2 * parts)
        part, column = divmod(inside, parts)
        part, column = 2 * part + column % 2, 2 * pair + column // 2
        goal = down_ref.at[part * half : (part + 1) * half, :, column * LANES : (column + 1) * LANES]
        goal[...] = tiles_ref[third + place // 2, place % 2]
    stores[5].start()
    for kind in (0, 2):
        for column in range(third * 2 * (half // rows)):
            place, part = divmod(column, half // rows)
            goal, at = up_ref, column
            if kind == 2:
                goal, at = (out_ref, column) if column < out_columns else (proj_ref, column - out_columns)
            source = tiles_ref[kind * third + place // 2, place % 2, part * rows : (part + 1) * rows]
            goal[:, :, at * LANES : (at + 1) * LANES] = source
        for store in stores[2:4] if kind else stores[4:5]:
            store.start()
    for store in stores:
        store.wait()


def place_results(dp_size, hidden, output, tokens_grad, final, bias):
    f32 = jnp.float32
    width = output.shape[1]
    rows = width // dp_size
    tile_rows = rows // SUBLANES
    shape = jax.ShapeDtypeStruct
    anywhere, vmem = pl.BlockSpec(memory_space=pl.ANY), pl.BlockSpec(memory_space=pltpu.VMEM)
    large = (
        (output.shape, output.dtype),
        (tokens_grad.shape, f32),
        ((tile_rows, SUBLANES, 3 * width), f32),
        ((tile_rows, SUBLANES, width), f32),
        ((tile_rows, SUBLANES, hidden), f32),
        ((hidden // dp_size // SUBLANES, SUBLANES, width), f32),
    )
    vectors = (((rows,), f32),) * len(NARROW) + (((hidden // dp_size,), f32),)
    return pl.pallas_call(
        place_kernel,
        out_shape=tuple(shape(*one) for one in large + vectors),
        in_specs=[vmem] * 4,
        out_specs=(anywhere,) * len(large + vectors),
        scratch_shapes=[pltpu.VMEM(*one) for one in large[2:] + vectors]
        + [pltpu.SemaphoreType.DMA((len(large + vectors),))],
        compiler_params=pltpu.CompilerParams(vmem_limit_bytes=16 * 2**20),
    )(output, tokens_grad, final, bias)


def ring_shards(*arrays):
    group_size, dp_size = lax.axis_size("group"), lax.axis_size("dp")
    tokens = arrays[0]
    _, token_count, width = tokens.shape
    hidden = arrays[14].shape[1]
    slots = float(dp_size * (group_size // 2) * token_count)
    flat = [tokens[0], arrays[1][0], *arrays[2:]]
    placed = place_results(dp_size, hidden, *layer(group_size, dp_size, slots, flat))
    output, tokens_grad, proj, out, up, down = placed[:6]
    narrow = dict(zip(NARROW, placed[6:14]))
    rows = width // dp_size
    return (
        output[None],
        tokens_grad[None],
        proj.reshape(rows, 3 * width),
        narrow["query"],
        narrow["value"],
        out.reshape(rows, width),
        narrow["out"],
        narrow["gain1"],
        narrow["shift1"],
        narrow["gain2"],
        narrow["shift2"],
        up.reshape(rows, hidden),
        placed[14],
        down.reshape(hidden // dp_size, width),
        narrow["down"],
    )


def solution(mesh):
    in_specs = (
        P(("group", "dp"), None, None),
        P(("group", "dp"), None, None),
        P(),
        P(("group", "dp")),
        P(("group", "dp"), None),
        P(),
        P(),
        P(),
        P(),
        P(),
        P(),
        P(),
        P(),
        P(),
        P(),
        P(),
        P(),
        P(),
    )
    out_specs = (
        P(("group", "dp"), None, None),
        P(("group", "dp"), None, None),
        P("dp", None),
        P("dp"),
        P("dp"),
        P("dp", None),
        P("dp"),
        P("dp"),
        P("dp"),
        P("dp"),
        P("dp"),
        P("dp", None),
        P("dp"),
        P("dp", None),
        P("dp"),
    )
    group_size, dp_size = mesh.shape["group"], mesh.shape["dp"]

    def body(*arrays):
        tokens, out_weight, up_weight = arrays[0], arrays[8], arrays[14]
        whole_tiles = (out_weight.shape[0] // dp_size) % SUBLANES == 0
        one_row = tokens.shape[:2] == (1, 512) and up_weight.shape == (768, 3072)
        powers = group_size == 4 and dp_size >= 4 and dp_size & (dp_size - 1) == 0
        return (ring_shards if whole_tiles and one_row and powers else plain_shards)(*arrays)

    return jax.shard_map(body, mesh=mesh, in_specs=in_specs, out_specs=out_specs, check_vma=False)
```
